256 devices in a mesh: snap: 4 (over x), cell: 64 (over z, y, core).
Axes of the slice: x: 4, y: 4, z: 8, core: 2. Of those that a mesh axis runs over, the one named last changes fastest.
Arguments:
- start_states: float32 [1024, 131072], P('snap', 'cell'), may hold values from -6 to 6
- sources: bfloat16 [2, 1024, 131072], P(None, 'snap', 'cell'), may hold values from -40 to 40
- blocks: bfloat16 [2048, 64, 448], P('cell'), may hold values from -0.25 to 0.25
- columns: int32 [2048, 7], P('cell'), may hold values from 0 to 2047, as said below
- leaf_sketch: float32 [200, 512], replicated, may hold values from -1 to 2
- merge_sketch: float32 [2, 200, 400], replicated, may hold values from -1 to 2
Outputs:
- projected: float32 [1024, 131072], P('snap', 'cell')
The draws below stay inside these ranges and needn't reach their ends.
Inputs may be any that keep to these rules, and one draw needn't show every extreme that they name: columns[b, 0] = b, and every entry lies within 4 of b.
All inputs are finite; a program needn't handle non-finite values.
Results may differ from the reference program's by a relative error of at most 0.0014.
Values may be sent and summed in bfloat16 or wider, within the bound.
A program may use at most 128 MiB of HBM per device.

```python
import jax
import jax.numpy as jnp
from jax import lax

BLOCK = 64
NNZ = 7
HB = 4
RANK = 200
STEPS = 2
M = 256
NBT = 2048
NC = 131072
SNAP_ROWS = 1024
N_SNAP = 4


def draw_sources(key, part):
    noise_key, rough_key = jax.random.split(jax.random.fold_in(key, 11))
    position = jnp.arange(NC, dtype=jnp.float32) / NC
    rough = jax.random.uniform(rough_key, (NC,), jnp.float32, 0.5, 2.0)
    amplitude = jnp.exp(jnp.log(3.0) * position) * rough
    shape = (STEPS, SNAP_ROWS, NC)
    values = jnp.clip(jax.random.normal(noise_key, shape, jnp.float32), -6.0, 6.0) * amplitude
    return values.astype(jnp.bfloat16)


def draw_columns(key, part):
    offsets = jax.random.randint(jax.random.fold_in(key, 23), (NBT, NNZ), -HB, HB + 1)
    slot = jnp.arange(NNZ, dtype=jnp.int32)[None, :]
    offsets = jnp.where(slot == 0, 0, offsets)
    rowid = jnp.arange(NBT, dtype=jnp.int32)[:, None]
    return jnp.clip(rowid + offsets, 0, NBT - 1).astype(jnp.int32)


def sketch_noise(key, shape, fan):
    values = jnp.clip(jax.random.normal(key, shape, jnp.float32), -4.0, 4.0)
    return 0.5 * values / jnp.sqrt(jnp.float32(fan))


def draw_leaf_sketch(key, part):
    noise = sketch_noise(jax.random.fold_in(key, 37), (RANK, STEPS * M), STEPS * M)
    return jnp.eye(RANK, STEPS * M, dtype=jnp.float32) + noise


def draw_merge_sketch(key, part):
    noise = sketch_noise(jax.random.fold_in(key, 41), (2, RANK, 2 * RANK), 2 * RANK)
    eye_pair = jnp.concatenate([jnp.eye(RANK, dtype=jnp.float32), jnp.eye(RANK, dtype=jnp.float32)], axis=1)
    return eye_pair[None, :, :] + noise


def levels(key, dims, cuts, low, top_value):
    loudness = 1.0
    for axis_at, shards_of in cuts:
        heights = jax.random.uniform(jax.random.fold_in(jax.random.fold_in(key, 6), axis_at), (shards_of,), jnp.float32, low / len(cuts), top_value / len(cuts))
        loudness = loudness * jnp.repeat(jnp.exp(heights), dims[axis_at] // shards_of).reshape((-1,) + (1,) * (len(dims) - 1 - axis_at))
    return loudness


def centred(rng, extent, deviation, reach, shards=(), held_as=jnp.bfloat16):
    drawn = deviation * jax.random.normal(rng, extent, jnp.float32)
    if shards:
        drawn = drawn * levels(rng, extent, shards, -0.22, 0.18)
    return jnp.clip(drawn, -reach, reach).astype(held_as)


def setup_inputs(seed: int = 0) -> dict:
    streams_of = jax.random.split(jax.random.key(seed), 7)
    start_states = centred(streams_of[0], (SNAP_ROWS, NC), 1.0, 6.0, ((0, 4), (1, 64)), jnp.float32)
    sources = draw_sources(jax.random.fold_in(streams_of[6], 71), 0)
    blocks = centred(streams_of[2], (NBT, BLOCK, NNZ * BLOCK), (NNZ * BLOCK) ** -0.5, 0.25, ((0, 64),))
    columns = draw_columns(jax.random.fold_in(streams_of[6], 71), 0)
    leaf_sketch = draw_leaf_sketch(jax.random.fold_in(streams_of[6], 71), 0)
    merge_sketch = draw_merge_sketch(jax.random.fold_in(streams_of[6], 71), 0)
    return {"start_states": start_states, "sources": sources, "blocks": blocks, "columns": columns, "leaf_sketch": leaf_sketch, "merge_sketch": merge_sketch}


def apply_op(state, blocks, columns):
    rows = state.shape[0]
    xb = state.astype(jnp.bfloat16).reshape(rows, NBT, BLOCK)
    picked = jnp.take(xb, columns.reshape(-1), axis=1).reshape(rows, NBT, NNZ * BLOCK)
    result = jnp.einsum('mbk,brk->mbr', picked.astype(jnp.float32), blocks.astype(jnp.float32), precision=lax.Precision.HIGHEST)
    return result.reshape(rows, NC)

def orth(z_rows):
    gram = jnp.dot(z_rows, z_rows.T, precision=lax.Precision.HIGHEST)
    lower = jnp.linalg.cholesky(gram)
    return lax.linalg.triangular_solve(lower, z_rows, left_side=True, lower=True)

def merge(sketch, first, second):
    return jnp.dot(sketch[:, :RANK], first, precision=lax.Precision.HIGHEST) + jnp.dot(sketch[:, RANK:], second, precision=lax.Precision.HIGHEST)

def reference(start_states, sources, blocks, columns, leaf_sketch, merge_sketch):
    leaves = []
    finals = []
    for group in range(N_SNAP):
        state = start_states[group * M:(group + 1) * M]
        snaps = []
        for step in range(STEPS):
            state = state - apply_op(state, blocks, columns) + sources[step, group * M:(group + 1) * M].astype(jnp.float32)
            snaps.append(state)
        stacked = jnp.concatenate(snaps, axis=0)
        leaves.append(orth(jnp.dot(leaf_sketch, stacked, precision=lax.Precision.HIGHEST)))
        finals.append(state)
    pair_low = orth(merge(merge_sketch[0], leaves[0], leaves[1]))
    pair_high = orth(merge(merge_sketch[0], leaves[2], leaves[3]))
    basis = orth(merge(merge_sketch[1], pair_low, pair_high))
    outputs = []
    for group in range(N_SNAP):
        coeffs = jnp.dot(finals[group], basis.T, precision=lax.Precision.HIGHEST)
        outputs.append(jnp.dot(coeffs, basis, precision=lax.Precision.HIGHEST))
    return jnp.concatenate(outputs, axis=0)
```

```python
import jax
import jax.numpy as jnp
from jax import lax
from jax.experimental import pallas as pl
from jax.experimental.pallas import tpu as pltpu
from jax.sharding import PartitionSpec as P

HB = 4
NZ = 8
NW = 8
NX = 4
NB = 40
MESH = pl.DeviceIdType.MESH
F32 = jnp.float32
BF16 = jnp.bfloat16


def mm(a, b):
    return jnp.dot(a, b, precision=lax.Precision.HIGHEST, preferred_element_type=F32)


def mm_nt(a, b):
    return lax.dot_general(
        a, b, (((1,), (1,)), ((), ())), precision=lax.Precision.HIGHEST, preferred_element_type=F32
    )


def mm_tn(a, b):
    return lax.dot_general(
        a, b, (((0,), (0,)), ((), ())), precision=lax.Precision.HIGHEST, preferred_element_type=F32
    )


def snap_kernel(
    x0_ref, src_ref, blk_ref, cols_ref, sk_ref,
    x2_ref, y_ref, g_ref,
    x1_ref, dup_a, dup_b, out_h, in_h, send_sem, recv_sem,
):
    x = lax.axis_index("snap")
    c = lax.axis_index("cell")
    n = 64
    left, right = lax.rem(c + n - 1, n), lax.rem(c + 1, n)
    barrier = pltpu.get_barrier_semaphore()
    for peer in (left, right):
        pl.semaphore_signal(barrier, inc=1, device_id=(x, peer), device_id_type=MESH)
    rows = x0_ref.shape[0]
    npair = x0_ref.shape[1] // 128
    low = lax.broadcasted_iota(jnp.int32, (rows, 128), 1) < 64

    def spread(tile, dup, p):
        turned = pltpu.roll(tile, 64, axis=1)
        dup[2 * p] = jnp.where(low, tile, turned).astype(BF16)
        dup[2 * p + 1] = jnp.where(low, turned, tile).astype(BF16)

    def lanes(p):
        return pl.ds(pl.multiple_of(p * 128, 128), 128)

    def copies(step):
        return [
            pltpu.make_async_remote_copy(
                src_ref=out_h.at[step, pl.ds(2 * side, 2)],
                dst_ref=in_h.at[step, pl.ds(2 - 2 * side, 2)],
                send_sem=send_sem.at[step, side],
                recv_sem=recv_sem.at[step, side],
                device_id=(x, peer),
                device_id_type=MESH,
            )
            for side, peer in ((0, left), (1, right))
        ]

    def apply(dup, xin, xout, s, p, then):
        halves = []
        for b2 in range(2):
            b = 2 * p + b2
            parts = []
            for jj in range(3):
                ca = cols_ref[b, 2 * jj]
                cb = cols_ref[b, 2 * jj + 1]
                parts.append(jnp.where(low, dup[ca], dup[cb]))
            parts.append(dup[cols_ref[b, 6]][:, :64])
            picked = jnp.concatenate(parts, axis=1)
            halves.append(
                lax.dot_general(
                    picked, blk_ref[b], (((1,), (1,)), ((), ())), preferred_element_type=F32
                )
            )
        res = jnp.concatenate(halves, axis=1)
        new = xin[:, lanes(p)] - res + src_ref[s, :, lanes(p)].astype(F32)
        xout[:, lanes(p)] = new
        if then is not None:
            spread(new, then, p + 2)
        return new

    for e in range(2):
        out_h[0, e] = x0_ref[:, e * 128 : (e + 1) * 128].astype(BF16)
        q = npair - 2 + e
        out_h[0, 2 + e] = x0_ref[:, q * 128 : (q + 1) * 128].astype(BF16)
    pl.semaphore_wait(barrier, 2)
    first = copies(0)
    for cp in first:
        cp.start()

    @pl.loop(0, npair)
    def _(p):
        spread(x0_ref[:, lanes(p)], dup_a, p + 2)

    @pl.loop(2, npair - 2)
    def _(p):
        apply(dup_a, x0_ref, x1_ref, 0, p, dup_b)

    def arrive(step, dup):
        for e in range(2):
            spread(in_h[step, e].astype(F32), dup, e)
            spread(in_h[step, 2 + e].astype(F32), dup, npair + 2 + e)

    for cp in first:
        cp.wait()
    arrive(0, dup_a)
    for e, p in enumerate((0, 1, npair - 2, npair - 1)):
        out_h[1, e] = apply(dup_a, x0_ref, x1_ref, 0, p, dup_b).astype(BF16)
    second = copies(1)
    for cp in second:
        cp.start()

    @pl.loop(2, npair - 2)
    def _(p):
        apply(dup_b, x1_ref, x2_ref, 1, p, None)

    for cp in second:
        cp.wait()
    arrive(1, dup_b)
    for p in (0, 1, npair - 2, npair - 1):
        apply(dup_b, x1_ref, x2_ref, 1, p, None)

    for q in range(4):
        cut = slice(q * 512, (q + 1) * 512)
        y_ref[q] = mm(sk_ref[:, :rows], x1_ref[:, cut]) + mm(sk_ref[:, rows:], x2_ref[:, cut])
        y = y_ref[q]
        g = mm_nt(y, y)
        if q == 0:
            g_ref[...] = g
        else:
            g_ref[...] += g


def snapshots(start_states, sources, blocks, cols, leaf_sketch):
    rows, width = start_states.shape
    rank = leaf_sketch.shape[0]
    nblk = width // 64
    vmem = pl.BlockSpec(memory_space=pltpu.VMEM)
    return pl.pallas_call(
        snap_kernel,
        name="snapshots",
        out_shape=(
            jax.ShapeDtypeStruct((rows, width), F32),
            jax.ShapeDtypeStruct((4, rank, width // 4), F32),
            jax.ShapeDtypeStruct((rank, rank), F32),
        ),
        in_specs=[vmem, vmem, vmem, pl.BlockSpec(memory_space=pltpu.SMEM), vmem],
        out_specs=(vmem, vmem, vmem),
        scratch_shapes=[
            pltpu.VMEM((rows, width), F32),
            pltpu.VMEM((nblk + 2 * HB, rows, 128), BF16),
            pltpu.VMEM((nblk + 2 * HB, rows, 128), BF16),
            pltpu.VMEM((2, 4, rows, 128), BF16),
            pltpu.VMEM((2, 4, rows, 128), BF16),
            pltpu.SemaphoreType.DMA((2, 2)),
            pltpu.SemaphoreType.DMA((2, 2)),
        ],
        compiler_params=pltpu.CompilerParams(
            collective_id=0, has_side_effects=True, vmem_limit_bytes=48 * 2**20
        ),
    )(start_states, sources, blocks, cols, leaf_sketch)


def eliminate(tiles):
    nt = len(tiles[0])
    sub = lax.broadcasted_iota(jnp.int32, (8, 128), 0)
    for t in range(nt):
        cols = [
            [
                [jnp.broadcast_to(r[u][:, 8 * t + j : 8 * t + j + 1], (8, 128)) for j in range(8)]
                for u in range(t, nt)
            ]
            for r in tiles
        ]
        for j in range(8):
            for r, cl in zip(tiles, cols):
                pivot = jnp.broadcast_to(cl[0][j][j : j + 1], (8, 128))
                inv = lax.rsqrt(pivot)
                row = jnp.broadcast_to(r[t][j : j + 1], (8, 128)) * inv
                heads = [jnp.broadcast_to(cl[0][j][m : m + 1], (8, 128)) * inv for m in range(j + 1, 8)]
                for u in range(t, nt):
                    lcol = cl[u - t][j] * inv
                    if u == t:
                        lcol = jnp.where(sub > j, lcol, 0.0)
                        r[u] = jnp.where(sub == j, row, r[u] - lcol * row)
                    else:
                        r[u] = r[u] - lcol * row
                    for m in range(j + 1, 8):
                        cl[u - t][m] = cl[u - t][m] - lcol * heads[m - j - 1]
    return tiles


def chol_inv(a_ref, t_ref, batch):
    n = a_ref.shape[1]
    steps = n // NB
    r_io = lax.broadcasted_iota(jnp.int32, (n, 256), 0)
    c_io = lax.broadcasted_iota(jnp.int32, (n, 256), 1)
    eye = jnp.where(r_io == c_io, 1.0, 0.0).astype(F32)
    for b in range(batch):
        t_ref[b] = eye
    lane = lax.broadcasted_iota(jnp.int32, (NB, 128), 1)
    srow = lax.broadcasted_iota(jnp.int32, (NB, 128), 0)
    lane2 = lax.broadcasted_iota(jnp.int32, (NB, 256), 1)

    @pl.loop(0, steps)
    def _(k):
        rows = pl.ds(pl.multiple_of(k * NB, 8), NB)
        tiles = []
        for b in range(batch):
            blk = pltpu.roll(a_ref[b, rows, :], lax.rem(256 - k * NB, 256), axis=1)[:, :128]
            blk = jnp.where(lane < NB, blk, jnp.where(lane == 64 + srow, 1.0, 0.0))
            tiles.append([blk[8 * t : 8 * t + 8] for t in range(NB // 8)])
        tiles = eliminate(tiles)
        for b in range(batch):
            tk = pltpu.roll(jnp.concatenate(tiles[b], axis=0), 64, axis=1)[:, :NB]
            wa = mm(tk, a_ref[b, rows, :])
            wt = mm(tk, t_ref[b, rows, :])
            wm = jnp.where((lane2 >= (k + 1) * NB) & (lane2 < n), wa, 0.0)
            lt = wm.T[:n]
            a_ref[b] = a_ref[b] - mm(lt, wa)
            t_ref[b] = t_ref[b] - mm(lt, wt)
            t_ref[b, rows, :] = wt


def exchange(src_of, dst, count, me, device_of, send_sem, recv_sem):
    sends, waits = [], []
    for d in range(1, count):
        peer = lax.rem(me + d, count)
        cp = pltpu.make_async_remote_copy(
            src_ref=src_of(peer), dst_ref=dst.at[me], send_sem=send_sem.at[d], recv_sem=recv_sem.at[me],
            device_id=device_of(peer), device_id_type=MESH,
        )
        cp.start()
        sends.append(cp)
        origin = lax.rem(me + count - d, count)
        waits.append(
            pltpu.make_async_remote_copy(
                src_ref=src_of(peer), dst_ref=dst.at[origin], send_sem=send_sem.at[d], recv_sem=recv_sem.at[origin],
                device_id=device_of(peer), device_id_type=MESH,
            )
        )
    return sends, waits


def finish(pair):
    sends, waits = pair
    for w in waits:
        w.wait_recv()
    for s in sends:
        s.wait_send()


def add_up(ref, count):
    total = ref[0]
    for i in range(1, count):
        total = total + ref[i]
    return total


class Where:
    def __init__(self):
        self.x = lax.axis_index("snap")
        c = lax.axis_index("cell")
        self.z, self.w = c // NW, lax.rem(c, NW)

    def along_z(self, peer):
        return (self.x, peer * NW + self.w)

    def along_w(self, peer):
        return (self.x, self.z * NW + peer)

    def along_x(self, peer):
        return (peer, self.z * NW + self.w)


def reduce_all(at, pk, size, bufs, mode, between=None):
    r1, r2, rx, out, ss, rs = bufs

    def piece(peer):
        return pk.at[pl.ds(pl.multiple_of(peer * size, 8), size)]

    r1[at.z] = pk[pl.ds(pl.multiple_of(at.z * size, 8), size), :]
    finish(exchange(piece, r1, NZ, at.z, at.along_z, ss.at[0], rs.at[0]))
    r2[at.w] = add_up(r1, NZ)
    finish(exchange(lambda _: r2.at[at.w], r2, NW, at.w, at.along_w, ss.at[1], rs.at[1]))
    total = add_up(r2, NW)
    if mode == "cell":
        out[at.z] = total
    else:
        rx[at.x] = total
        finish(exchange(lambda _: rx.at[at.x], rx, NX, at.x, at.along_x, ss.at[2], rs.at[2]))
        out[at.z] = add_up(rx, NX) if mode == "sum" else rx[...]
    if between is not None:
        between()
    finish(exchange(lambda _: out.at[at.z], out, NZ, at.z, at.along_z, ss.at[3], rs.at[3]))


def pack(g, g_ref, pk, base):
    g_ref[:, : g.shape[1]] = g
    pk[base : base + 200, :] = g_ref[:, :128]
    pk[base + 200 : base + 272, :] = g_ref[128:200, 128:]


def unpack(pk, base, a_ref, b):
    a_ref[b, :, :128] = pk[base : base + 200, :]
    a_ref[b, 128:200, 128:] = pk[base + 200 : base + 272, :]
    a_ref[b, :128, 128:] = pk[base + 128 : base + 256, :].T


def merge_kernel(
    y_ref, g_ref, x2_ref, ms_ref,
    zf_ref, co_ref,
    yq, m_ref, gs, a4, t4, flat,
    pk1, l1, l2, lx, lo, pk2, p1, p2, px, po, pk3, c1, c2, co,
    s1, q1, s2, q2, s3, q3, sb, qb,
):
    at = Where()
    n = 200
    barrier = pltpu.get_barrier_semaphore()
    for d in range(1, NZ):
        pl.semaphore_signal(barrier, inc=1, device_id=at.along_z(lax.rem(at.z + d, NZ)), device_id_type=MESH)
        pl.semaphore_signal(barrier, inc=1, device_id=at.along_w(lax.rem(at.w + d, NW)), device_id_type=MESH)
    for d in range(1, NX):
        pl.semaphore_signal(barrier, inc=1, device_id=at.along_x(lax.rem(at.x + d, NX)), device_id_type=MESH)
    gs[...] = jnp.zeros_like(gs)
    pk1[...] = jnp.zeros_like(pk1)
    pk2[...] = jnp.zeros_like(pk2)
    pk3[...] = jnp.zeros_like(pk3)
    pack(g_ref[...], gs, pk1, 0)
    pl.semaphore_wait(barrier, 2 * (NZ - 1) + NX - 1)

    bulk = []

    def send_y():
        bulk.append(exchange(lambda peer: y_ref.at[peer], yq, NX, at.x, at.along_x, sb.at[0], qb.at[0]))

    reduce_all(at, pk1, 40, (l1, l2, lx, lo, s1, q1), "gather", between=send_y)
    yq[at.x] = y_ref[at.x]
    for g in range(NX):
        for o in range(NZ):
            flat[o * 40 : (o + 1) * 40, :] = lo[o, g]
        unpack(flat, 0, a4, g)
    chol_inv(a4, t4, NX)
    coef = [mm(ms_ref[0, :, n * (g % 2) : n * (g % 2) + n], t4[g][:, :n]) for g in range(NX)]
    finish(bulk[0])

    for p in range(2):
        m_ref[p] = mm(coef[2 * p], yq[2 * p]) + mm(coef[2 * p + 1], yq[2 * p + 1])
        pack(mm_nt(m_ref[p], m_ref[p]), gs, pk2, 272 * p)
    reduce_all(at, pk2, 72, (p1, p2, px, po, s2, q2), "sum")
    for o in range(NZ):
        flat[o * 72 : (o + 1) * 72, :] = po[o]
    for p in range(2):
        unpack(flat, 272 * p, a4, p)
    chol_inv(a4, t4, 2)
    z = mm(mm(ms_ref[1, :, :n], t4[0][:, :n]), m_ref[0]) + mm(mm(ms_ref[1, :, n:], t4[1][:, :n]), m_ref[1])

    zf_ref[at.x] = z
    finish(exchange(lambda _: zf_ref.at[at.x], zf_ref, NX, at.x, at.along_x, sb.at[1], qb.at[1]))
    gram = mm_nt(zf_ref[0], zf_ref[0])
    raw = mm_nt(x2_ref[:, :512], zf_ref[0])
    for q in range(1, NX):
        gram = gram + mm_nt(zf_ref[q], zf_ref[q])
        raw = raw + mm_nt(x2_ref[:, q * 512 : (q + 1) * 512], zf_ref[q])
    pack(gram, gs, pk3, 512)
    pk3[0:256, :] = raw[:, :128]
    pk3[256:512, :72] = raw[:, 128:]
    reduce_all(at, pk3, 104, (c1, c2, None, co, s3, q3), "cell")
    for o in range(NZ):
        flat[o * 104 : (o + 1) * 104, :] = co[o]
    unpack(flat, 512, a4, 0)
    chol_inv(a4, t4, 1)
    t = t4[0][:, :n]
    first = mm_nt(flat[0:256, :], t[:, :128]) + mm_nt(flat[256:512, :][:, :72], t[:, 128:])
    co_ref[...] = mm(first, t)


def merged(y, g, x2, merge_sketch):
    rank = y.shape[1]
    part = y.shape[2]
    rows = x2.shape[0]
    vmem = pl.BlockSpec(memory_space=pltpu.VMEM)
    dma = pltpu.SemaphoreType.DMA

    def buf(*shape):
        return pltpu.VMEM(shape, F32)

    return pl.pallas_call(
        merge_kernel,
        name="merge",
        out_shape=(
            jax.ShapeDtypeStruct((NX, rank, part), F32),
            jax.ShapeDtypeStruct((rows, rank), F32),
        ),
        in_specs=[vmem] * 4,
        out_specs=(vmem, vmem),
        scratch_shapes=[
            buf(NX, rank, part), buf(2, rank, part), buf(rank, 256), buf(NX, rank, 256), buf(NX, rank, 256),
            buf(832, 128),
            buf(320, 128), buf(NZ, 40, 128), buf(NW, 40, 128), buf(NX, 40, 128), buf(NZ, NX, 40, 128),
            buf(576, 128), buf(NZ, 72, 128), buf(NW, 72, 128), buf(NX, 72, 128), buf(NZ, 72, 128),
            buf(832, 128), buf(NZ, 104, 128), buf(NW, 104, 128), buf(NZ, 104, 128),
            dma((4, 8)), dma((4, 8)), dma((4, 8)), dma((4, 8)), dma((4, 8)), dma((4, 8)), dma((2, 4)), dma((2, 4)),
        ],
        compiler_params=pltpu.CompilerParams(
            collective_id=1, has_side_effects=True, vmem_limit_bytes=48 * 2**20
        ),
    )(y, g, x2, merge_sketch)


def project_kernel(co_ref, z_ref, o_ref):
    o_ref[...] = mm(co_ref[...], z_ref[0])


def project(coeffs, z):
    rows, rank = coeffs.shape
    parts, _, part = z.shape
    return pl.pallas_call(
        project_kernel,
        name="project",
        grid=(parts,),
        out_shape=jax.ShapeDtypeStruct((rows, parts * part), F32),
        in_specs=[
            pl.BlockSpec((rows, rank), lambda q: (0, 0)),
            pl.BlockSpec((1, rank, part), lambda q: (q, 0, 0)),
        ],
        out_specs=pl.BlockSpec((rows, part), lambda q: (0, q)),
        compiler_params=pltpu.CompilerParams(vmem_limit_bytes=32 * 2**20),
    )(coeffs, z)


def local(start_states, sources, blocks, columns, leaf_sketch, merge_sketch):
    cols = columns - lax.axis_index("cell") * blocks.shape[0] + HB
    x2, y, g = snapshots(start_states, sources, blocks, cols, leaf_sketch)
    z, coeffs = merged(y, g, x2, merge_sketch)
    return project(coeffs, z)


def solution(mesh):
    placed = (
        P("snap", "cell"),
        P(None, "snap", "cell"),
        P("cell", None, None),
        P("cell", None),
        P(),
        P(),
    )
    return jax.shard_map(
        local, mesh=mesh, in_specs=placed, out_specs=P("snap", "cell"), check_vma=False
    )
```

```python
import jax
import jax.numpy as jnp
from jax import lax
from jax.experimental import pallas as pl
from jax.experimental.pallas import tpu as pltpu
from jax.sharding import PartitionSpec as P

HB = 4
NZ = 8
NW = 8
NX = 4
NB = 40
MESH = pl.DeviceIdType.MESH
F32 = jnp.float32
BF16 = jnp.bfloat16


def mm(a, b):
    return jnp.dot(a, b, precision=lax.Precision.HIGHEST, preferred_element_type=F32)


def halves(a):
    high = a.astype(BF16)
    return high, (a - high.astype(F32)).astype(BF16)


def mm3(a, b):
    ah, al = halves(a)
    bh, bl = halves(b)
    small = jnp.dot(ah, bl, preferred_element_type=F32) + jnp.dot(al, bh, preferred_element_type=F32)
    return jnp.dot(ah, bh, preferred_element_type=F32) + small


def mm_nt(a, b):
    return lax.dot_general(
        a, b, (((1,), (1,)), ((), ())), precision=lax.Precision.HIGHEST, preferred_element_type=F32
    )


def eliminate(tiles):
    nt = len(tiles[0])
    sub = lax.broadcasted_iota(jnp.int32, (8, 128), 0)
    for t in range(nt):
        cols = [
            [
                [jnp.broadcast_to(r[u][:, 8 * t + j : 8 * t + j + 1], (8, 128)) for j in range(8)]
                for u in range(t, nt)
            ]
            for r in tiles
        ]
        for j in range(8):
            for r, cl in zip(tiles, cols):
                pivot = jnp.broadcast_to(cl[0][j][j : j + 1], (8, 128))
                inv = lax.rsqrt(pivot)
                row = jnp.broadcast_to(r[t][j : j + 1], (8, 128)) * inv
                heads = [jnp.broadcast_to(cl[0][j][m : m + 1], (8, 128)) * inv for m in range(j + 1, 8)]
                for u in range(t, nt):
                    lcol = cl[u - t][j] * inv
                    if u == t:
                        lcol = jnp.where(sub > j, lcol, 0.0)
                        r[u] = jnp.where(sub == j, row, r[u] - lcol * row)
                    else:
                        r[u] = r[u] - lcol * row
                    for m in range(j + 1, 8):
                        cl[u - t][m] = cl[u - t][m] - lcol * heads[m - j - 1]
    return tiles


def chol_inv(a_ref, batch, hooks=()):
    n = a_ref.shape[1]
    lane = lax.broadcasted_iota(jnp.int32, (NB, 128), 1)
    srow = lax.broadcasted_iota(jnp.int32, (NB, 128), 0)
    lane2 = lax.broadcasted_iota(jnp.int32, (NB, 256), 1)
    srow2 = lax.broadcasted_iota(jnp.int32, (NB, 256), 0)
    lane3 = lax.broadcasted_iota(jnp.int32, (n, 256), 1)
    srow3 = lax.broadcasted_iota(jnp.int32, (n, 256), 0)

    def step(k):
        lo = k * NB
        hi = lo + NB
        rows = pl.ds(pl.multiple_of(lo, 8), NB)
        tiles = []
        for b in range(batch):
            blk = pltpu.roll(a_ref[b, rows, :], lax.rem(256 - lo, 256), axis=1)[:, :128]
            blk = jnp.where(lane < NB, blk, jnp.where(lane == 64 + srow, 1.0, 0.0))
            tiles.append([blk[8 * t : 8 * t + 8] for t in range(NB // 8)])
        tiles = eliminate(tiles)
        for b in range(batch):
            tk = pltpu.roll(jnp.concatenate(tiles[b], axis=0), 64, axis=1)[:, :NB]
            own = jnp.where(lane2 - lo == srow2, 1.0, 0.0)
            w = mm(tk, jnp.where((lane2 >= lo) & (lane2 < hi), own, a_ref[b, rows, :]))
            lt = jnp.where((lane2 >= hi) & (lane2 < n), w, 0.0).T[:n]
            rest = jnp.where((lane3 >= lo) & (lane3 < hi) & (srow3 >= hi), 0.0, a_ref[b])
            a_ref[b] = rest - mm(lt, w)
            a_ref[b, rows, :] = jnp.where(lane2 < hi, w, 0.0)

    at = 0
    for stop, call in (*hooks, (n // NB, None)):
        pl.loop(at, stop)(step)
        if call is not None:
            call()
        at = stop


def exchange(src_of, dst, count, me, device_of, send_sem, recv_sem):
    sends, waits = [], []
    for d in range(1, count):
        peer = lax.rem(me + d, count)
        cp = pltpu.make_async_remote_copy(
            src_ref=src_of(peer), dst_ref=dst.at[me], send_sem=send_sem.at[d], recv_sem=recv_sem.at[me],
            device_id=device_of(peer), device_id_type=MESH,
        )
        cp.start()
        sends.append(cp)
        origin = lax.rem(me + count - d, count)
        waits.append(
            pltpu.make_async_remote_copy(
                src_ref=src_of(peer), dst_ref=dst.at[origin], send_sem=send_sem.at[d], recv_sem=recv_sem.at[origin],
                device_id=device_of(peer), device_id_type=MESH,
            )
        )
    return sends, waits


def finish(pair):
    sends, waits = pair
    for w in waits:
        w.wait_recv()
    for s in sends:
        s.wait_send()


def add_up(ref, count):
    total = ref[0]
    for i in range(1, count):
        total = total + ref[i]
    return total


class Where:
    def __init__(self):
        self.x = lax.axis_index("snap")
        self.c = lax.axis_index("cell")
        self.z, self.w = self.c // NW, lax.rem(self.c, NW)

    def along_z(self, peer):
        return (self.x, peer * NW + self.w)

    def along_w(self, peer):
        return (self.x, self.z * NW + peer)

    def along_x(self, peer):
        return (peer, self.z * NW + self.w)


def reduce_steps(at, pk, size, bufs, over_snap):
    r1, r2, rx, out, ss, rs = bufs

    def piece(peer):
        return pk.at[pl.ds(pl.multiple_of(peer * size, 8), size)]

    going = exchange(piece, r1, NW, at.w, at.along_w, ss.at[0], rs.at[0])
    r1[at.w] = pk[pl.ds(pl.multiple_of(at.w * size, 8), size), :]
    yield
    finish(going)
    r2[at.z] = add_up(r1, NW)
    going = exchange(lambda _: r2.at[at.z], r2, NZ, at.z, at.along_z, ss.at[1], rs.at[1])
    yield
    finish(going)
    total = add_up(r2, NZ)
    if over_snap:
        rx[at.x] = total
        going = exchange(lambda _: rx.at[at.x], rx, NX, at.x, at.along_x, ss.at[2], rs.at[2])
        yield
        finish(going)
        total = add_up(rx, NX)
    out[at.w] = total
    going = exchange(lambda _: out.at[at.w], out, NW, at.w, at.along_w, ss.at[3], rs.at[3])
    yield
    finish(going)


def run(steps):
    for _ in steps:
        pass


def pack(g, g_ref, pk, base):
    g_ref[:, : g.shape[1]] = g
    pk[base : base + 200, :] = g_ref[:, :128]
    pk[base + 200 : base + 272, :] = g_ref[128:200, 128:]


def unpack(pk, base, a_ref, b):
    a_ref[b, :, :128] = pk[base : base + 200, :]
    a_ref[b, 128:200, 128:] = pk[base + 200 : base + 272, :]
    a_ref[b, :128, 128:] = pk[base + 128 : base + 256, :].T


def main_kernel(
    x0_hbm, src_hbm, blk_hbm, cols_ref, sk_hbm, ms_hbm,
    zf_ref, co_ref,
    x0_ref, src_ref, blk_ref, sk_ref, ms_ref, x1_ref, x2_ref, y_ref, dup_a, dup_b, out_h, in_h,
    yq, m_ref, gs, u_ref, fac, tx, flat,
    pk1, l1, l2, lo, pk2, p1, p2, px, po, pk3, t1, t2, tw, to, pk4, c1, c2, co,
    in_sem, send_sem, recv_sem, s1, q1, s2, q2, s3, q3, s4, q4, sb, qb,
):
    at = Where()
    x, c = at.x, at.c
    n = 200
    ncell = NZ * NW
    loads = [
        pltpu.make_async_copy(src, dst, in_sem.at[i])
        for i, (src, dst) in enumerate(
            ((x0_hbm, x0_ref), (blk_hbm, blk_ref), (src_hbm, src_ref), (sk_hbm, sk_ref), (ms_hbm, ms_ref))
        )
    ]
    for ld in loads:
        ld.start()
    left, right = lax.rem(c + ncell - 1, ncell), lax.rem(c + 1, ncell)
    barrier = pltpu.get_barrier_semaphore()
    greeted = [(x, left), (x, right)]
    greeted += [at.along_z(lax.rem(at.z + d, NZ)) for d in range(1, NZ)]
    greeted += [at.along_w(lax.rem(at.w + d, NW)) for d in range(1, NW)]
    greeted += [at.along_x(lax.rem(at.x + d, NX)) for d in range(1, NX)]
    for device in greeted:
        pl.semaphore_signal(barrier, inc=1, device_id=device, device_id_type=MESH)

    rows = x0_ref.shape[0]
    npair = x0_ref.shape[1] // 128
    low = lax.broadcasted_iota(jnp.int32, (rows, 128), 1) < 64

    def spread(tile, dup, p):
        turned = pltpu.roll(tile, 64, axis=1)
        dup[2 * p] = jnp.where(low, tile, turned).astype(BF16)
        dup[2 * p + 1] = jnp.where(low, turned, tile).astype(BF16)

    def lanes(p):
        return pl.ds(pl.multiple_of(p * 128, 128), 128)

    def copies(step):
        return [
            pltpu.make_async_remote_copy(
                src_ref=out_h.at[step, pl.ds(2 * side, 2)],
                dst_ref=in_h.at[step, pl.ds(2 - 2 * side, 2)],
                send_sem=send_sem.at[step, side],
                recv_sem=recv_sem.at[step, side],
                device_id=(x, peer),
                device_id_type=MESH,
            )
            for side, peer in ((0, left), (1, right))
        ]

    def apply(dup, xin, xout, s, p, then):
        sides = []
        for b2 in range(2):
            b = 2 * p + b2
            parts = []
            for jj in range(3):
                ca = cols_ref[b, 2 * jj]
                cb = cols_ref[b, 2 * jj + 1]
                parts.append(jnp.where(low, dup[ca], dup[cb]))
            parts.append(dup[cols_ref[b, 6]][:, :64])
            picked = jnp.concatenate(parts, axis=1)
            sides.append(
                lax.dot_general(
                    picked, blk_ref[b], (((1,), (1,)), ((), ())), preferred_element_type=F32
                )
            )
        res = jnp.concatenate(sides, axis=1)
        new = xin[:, lanes(p)] - res + src_ref[s, :, lanes(p)].astype(F32)
        xout[:, lanes(p)] = new
        if then is not None:
            spread(new, then, p + 2)
        return new

    def arrive(step, dup):
        for e in range(2):
            spread(in_h[step, e].astype(F32), dup, e)
            spread(in_h[step, 2 + e].astype(F32), dup, npair + 2 + e)

    loads[0].wait()
    for e in range(2):
        out_h[0, e] = x0_ref[:, e * 128 : (e + 1) * 128].astype(BF16)
        q = npair - 2 + e
        out_h[0, 2 + e] = x0_ref[:, q * 128 : (q + 1) * 128].astype(BF16)
    pl.semaphore_wait(barrier, len(greeted))
    first = copies(0)
    for cp in first:
        cp.start()

    @pl.loop(0, npair)
    def _(p):
        spread(x0_ref[:, lanes(p)], dup_a, p + 2)

    for ld in loads[1:]:
        ld.wait()

    @pl.loop(2, npair - 2)
    def _(p):
        apply(dup_a, x0_ref, x1_ref, 0, p, dup_b)

    for cp in first:
        cp.wait()
    arrive(0, dup_a)
    for e, p in enumerate((0, 1, npair - 2, npair - 1)):
        out_h[1, e] = apply(dup_a, x0_ref, x1_ref, 0, p, dup_b).astype(BF16)
    second = copies(1)
    for cp in second:
        cp.start()

    @pl.loop(2, npair - 2)
    def _(p):
        apply(dup_b, x1_ref, x2_ref, 1, p, None)

    for cp in second:
        cp.wait()
    arrive(1, dup_b)
    for p in (0, 1, npair - 2, npair - 1):
        apply(dup_b, x1_ref, x2_ref, 1, p, None)

    gs[...] = jnp.zeros_like(gs)
    gram = None
    for q in range(NX):
        cut = slice(q * 512, (q + 1) * 512)
        y_ref[q] = mm3(sk_ref[:, :rows], x1_ref[:, cut]) + mm3(sk_ref[:, rows:], x2_ref[:, cut])
        part = mm_nt(y_ref[q], y_ref[q])
        gram = part if gram is None else gram + part

    pk1[272:, :] = jnp.zeros((48, 128), F32)
    pack(gram, gs, pk1, 0)
    steps = reduce_steps(at, pk1, 40, (l1, l2, None, lo, s1, q1), False)
    next(steps)
    bulk = exchange(lambda peer: y_ref.at[peer], yq, NX, x, at.along_x, sb.at[0], qb.at[0])
    yq[x] = y_ref[x]
    run(steps)
    for o in range(NW):
        flat[o * 40 : (o + 1) * 40, :] = lo[o]
    unpack(flat, 0, fac, 0)
    chol_inv(fac.at[pl.ds(0, 1)], 1)
    tx[x, :200] = fac[0, :, :128]
    tx[x, 200:] = fac[0, 128:, 128:]
    share = exchange(lambda _: tx.at[x], tx, NX, x, at.along_x, sb.at[1], qb.at[1])
    pk2[544:, :] = jnp.zeros((32, 128), F32)
    pk3[272:, :] = jnp.zeros((48, 128), F32)
    pk4[256:, :] = jnp.zeros((256, 128), F32)
    finish(share)
    finish(bulk)

    for p in range(2):
        for h in range(2):
            g = 2 * p + h
            sketch = ms_ref[0, :, n * h : n * h + n]
            u_ref[g, :, :128] = mm(sketch, tx[g, :200])
            u_ref[g, :, 128:] = mm(sketch[:, 128:], tx[g, 200:])
        m_ref[p] = mm(u_ref[2 * p, :, :n], yq[2 * p]) + mm(u_ref[2 * p + 1, :, :n], yq[2 * p + 1])
        pack(mm_nt(m_ref[p], m_ref[p]), gs, pk2, 272 * p)
    run(reduce_steps(at, pk2, 72, (p1, p2, px, po, s2, q2), True))
    for o in range(NW):
        flat[o * 72 : (o + 1) * 72, :] = po[o]
    for p in range(2):
        unpack(flat, 272 * p, fac, p)
    chol_inv(fac, 2)
    z = mm(mm(ms_ref[1, :, :n], fac[0][:, :n]), m_ref[0]) + mm(mm(ms_ref[1, :, n:], fac[1][:, :n]), m_ref[1])

    zf_ref[x] = z
    bulk = exchange(lambda _: zf_ref.at[x], zf_ref, NX, x, at.along_x, sb.at[2], qb.at[2])
    pack(mm_nt(z, z), gs, pk3, 0)
    steps = reduce_steps(at, pk3, 40, (t1, t2, tw, to, s3, q3), True)
    for _ in range(4):
        next(steps)
    finish(bulk)
    raw = mm_nt(x2_ref[:, :512], zf_ref[0])
    for q in range(1, NX):
        raw = raw + mm_nt(x2_ref[:, q * 512 : (q + 1) * 512], zf_ref[q])
    pk4[0:256, :] = raw[:, :128]
    pk4[256:512, :72] = raw[:, 128:]
    last = reduce_steps(at, pk4, 64, (c1, c2, None, co, s4, q4), False)
    next(last)
    run(steps)
    for o in range(NW):
        flat[o * 40 : (o + 1) * 40, :] = to[o]
    unpack(flat, 0, fac, 0)
    chol_inv(fac.at[pl.ds(0, 1)], 1, ((3, lambda: next(last)),))
    t = fac[0]
    u_ref[0] = mm(t.T[:n], t)
    run(last)
    for o in range(NW):
        flat[o * 64 : (o + 1) * 64, :] = co[o]
    co_ref[...] = (mm(flat[0:256, :], u_ref[0, :128, :]) + mm(flat[256:512, :][:, :72], u_ref[0, 128:, :]))[:, :n]


def merged_top(start_states, sources, blocks, cols, leaf_sketch, merge_sketch):
    rows, width = start_states.shape
    rank = leaf_sketch.shape[0]
    part = width // NX
    nblk = width // 64
    anywhere = pl.BlockSpec(memory_space=pl.ANY)
    vmem = pl.BlockSpec(memory_space=pltpu.VMEM)
    dma = pltpu.SemaphoreType.DMA

    def buf(*shape, dtype=F32):
        return pltpu.VMEM(shape, dtype)

    return pl.pallas_call(
        main_kernel,
        name="merged_top",
        out_shape=(
            jax.ShapeDtypeStruct((NX, rank, part), F32),
            jax.ShapeDtypeStruct((rows, rank), F32),
        ),
        in_specs=[anywhere] * 3 + [pl.BlockSpec(memory_space=pltpu.SMEM)] + [anywhere] * 2,
        out_specs=(vmem, vmem),
        scratch_shapes=[
            buf(rows, width), buf(*sources.shape, dtype=BF16), buf(*blocks.shape, dtype=BF16),
            buf(*leaf_sketch.shape), buf(*merge_sketch.shape),
            buf(rows, width), buf(rows, width), buf(NX, rank, part),
            buf(nblk + 2 * HB, rows, 128, dtype=BF16), buf(nblk + 2 * HB, rows, 128, dtype=BF16),
            buf(2, 4, rows, 128, dtype=BF16), buf(2, 4, rows, 128, dtype=BF16),
            buf(NX, rank, part), buf(2, rank, part), buf(rank, 256), buf(NX, rank, 256), buf(2, rank, 256),
            buf(NX, 272, 128), buf(576, 128),
            buf(320, 128), buf(NW, 40, 128), buf(NZ, 40, 128), buf(NW, 40, 128),
            buf(576, 128), buf(NW, 72, 128), buf(NZ, 72, 128), buf(NX, 72, 128), buf(NW, 72, 128),
            buf(320, 128), buf(NW, 40, 128), buf(NZ, 40, 128), buf(NX, 40, 128), buf(NW, 40, 128),
            buf(512, 128), buf(NW, 64, 128), buf(NZ, 64, 128), buf(NW, 64, 128),
            dma((5,)), dma((2, 2)), dma((2, 2)),
            dma((4, 8)), dma((4, 8)), dma((4, 8)), dma((4, 8)), dma((4, 8)), dma((4, 8)), dma((4, 8)), dma((4, 8)),
            dma((3, 4)), dma((3, 4)),
        ],
        compiler_params=pltpu.CompilerParams(
            collective_id=0, has_side_effects=True, vmem_limit_bytes=48 * 2**20
        ),
    )(start_states, sources, blocks, cols, leaf_sketch, merge_sketch)


def project_kernel(co_ref, z_ref, o_ref):
    o_ref[...] = mm3(co_ref[...], z_ref[0])


def project(coeffs, z):
    rows, rank = coeffs.shape
    parts, _, part = z.shape
    return pl.pallas_call(
        project_kernel,
        name="project",
        grid=(parts,),
        out_shape=jax.ShapeDtypeStruct((rows, parts * part), F32),
        in_specs=[
            pl.BlockSpec((rows, rank), lambda q: (0, 0)),
            pl.BlockSpec((1, rank, part), lambda q: (q, 0, 0)),
        ],
        out_specs=pl.BlockSpec((rows, part), lambda q: (0, q)),
        compiler_params=pltpu.CompilerParams(vmem_limit_bytes=32 * 2**20),
    )(coeffs, z)


def local(start_states, sources, blocks, columns, leaf_sketch, merge_sketch):
    cols = columns - lax.axis_index("cell") * blocks.shape[0] + HB
    z, coeffs = merged_top(start_states, sources, blocks, cols, leaf_sketch, merge_sketch)
    return project(coeffs, z)


def solution(mesh):
    placed = (
        P("snap", "cell"),
        P(None, "snap", "cell"),
        P("cell", None, None),
        P("cell", None),
        P(),
        P(),
    )
    return jax.shard_map(
        local, mesh=mesh, in_specs=placed, out_specs=P("snap", "cell"), check_vma=False
    )
```

```python
import jax
import jax.numpy as jnp
from jax import lax
from jax.experimental import pallas as pl
from jax.experimental.pallas import tpu as pltpu
from jax.sharding import PartitionSpec as P

HB = 4
NZ = 8
NW = 8
NX = 4
NB = 40
MESH = pl.DeviceIdType.MESH
F32 = jnp.float32
BF16 = jnp.bfloat16


def mm(a, b):
    return jnp.dot(a, b, precision=lax.Precision.HIGHEST, preferred_element_type=F32)


def halves(a):
    high = a.astype(BF16)
    return high, (a - high.astype(F32)).astype(BF16)


def mm3(a, b):
    ah, al = halves(a)
    bh, bl = halves(b)
    small = jnp.dot(ah, bl, preferred_element_type=F32) + jnp.dot(al, bh, preferred_element_type=F32)
    return jnp.dot(ah, bh, preferred_element_type=F32) + small


def mm_nt(a, b):
    return lax.dot_general(
        a, b, (((1,), (1,)), ((), ())), precision=lax.Precision.HIGHEST, preferred_element_type=F32
    )


def eliminate(tiles):
    nt = len(tiles[0])
    sub = lax.broadcasted_iota(jnp.int32, (8, 128), 0)
    for t in range(nt):
        cols = [
            [
                [jnp.broadcast_to(r[u][:, 8 * t + j : 8 * t + j + 1], (8, 128)) for j in range(8)]
                for u in range(t, nt)
            ]
            for r in tiles
        ]
        for j in range(8):
            for r, cl in zip(tiles, cols):
                pivot = jnp.broadcast_to(cl[0][j][j : j + 1], (8, 128))
                inv = lax.rsqrt(pivot)
                row = jnp.broadcast_to(r[t][j : j + 1], (8, 128)) * inv
                heads = [jnp.broadcast_to(cl[0][j][m : m + 1], (8, 128)) * inv for m in range(j + 1, 8)]
                for u in range(t, nt):
                    lcol = cl[u - t][j] * inv
                    if u == t:
                        lcol = jnp.where(sub > j, lcol, 0.0)
                        r[u] = jnp.where(sub == j, row, r[u] - lcol * row)
                    else:
                        r[u] = r[u] - lcol * row
                    for m in range(j + 1, 8):
                        cl[u - t][m] = cl[u - t][m] - lcol * heads[m - j - 1]
    return tiles


def chol_inv(a_ref, batch, after=None):
    n = a_ref.shape[1]
    lane = lax.broadcasted_iota(jnp.int32, (NB, 128), 1)
    srow = lax.broadcasted_iota(jnp.int32, (NB, 128), 0)
    lane2 = lax.broadcasted_iota(jnp.int32, (NB, 256), 1)
    srow2 = lax.broadcasted_iota(jnp.int32, (NB, 256), 0)
    for k in range(n // NB):
        lo = k * NB
        hi = lo + NB
        tiles = []
        for b in range(batch):
            blk = a_ref[b, lo:hi, :]
            if lo:
                blk = pltpu.roll(blk, 256 - lo, axis=1)
            blk = jnp.where(lane < NB, blk[:, :128], jnp.where(lane == 64 + srow, 1.0, 0.0))
            tiles.append([blk[8 * t : 8 * t + 8] for t in range(NB // 8)])
        tiles = eliminate(tiles)
        for b in range(batch):
            tk = pltpu.roll(jnp.concatenate(tiles[b], axis=0), 64, axis=1)[:, :NB]
            own = jnp.where(lane2 - lo == srow2, 1.0, 0.0)
            w = mm(tk, jnp.where((lane2 >= lo) & (lane2 < hi), own, a_ref[b, lo:hi, :]))
            if hi < n:
                lane3 = lax.broadcasted_iota(jnp.int32, (n - hi, 256), 1)
                rest = jnp.where((lane3 >= lo) & (lane3 < hi), 0.0, a_ref[b, hi:, :])
                a_ref[b, hi:, :] = rest - mm(w.T[hi:n], w)
            a_ref[b, lo:hi, :] = jnp.where(lane2 < hi, w, 0.0)
        if after is not None:
            after(k)


def exchange(src_of, dst_of, count, me, device_of, send_sem, recv_sem):
    sends, waits = [], []
    for d in range(1, count):
        peer = lax.rem(me + d, count)
        origin = lax.rem(me + count - d, count)

        def copy(slot, peer=peer, d=d):
            return pltpu.make_async_remote_copy(
                src_ref=src_of(peer), dst_ref=dst_of(slot), send_sem=send_sem.at[d], recv_sem=recv_sem.at[slot],
                device_id=device_of(peer), device_id_type=MESH,
            )

        cp = copy(me)
        cp.start()
        sends.append(cp)
        waits.append(copy(origin))
    return sends, waits


def finish(pair):
    sends, waits = pair
    for w in waits:
        w.wait_recv()
    for s in sends:
        s.wait_send()


def add_up(ref, count):
    total = ref[0]
    for i in range(1, count):
        total = total + ref[i]
    return total


class Where:
    def __init__(self):
        self.x = lax.axis_index("snap")
        self.c = lax.axis_index("cell")
        self.z, self.w = self.c // NW, lax.rem(self.c, NW)

    def along_z(self, peer):
        return (self.x, peer * NW + self.w)

    def along_w(self, peer):
        return (self.x, self.z * NW + peer)

    def along_x(self, peer):
        return (peer, self.z * NW + self.w)


def reduce_steps(at, pk, size, bufs, over_snap):
    r1, r2, rx, out, ss, rs = bufs

    def piece(ref):
        return lambda i: ref.at[pl.ds(pl.multiple_of(i * size, 8), size)]

    def mine(ref):
        return lambda i: ref.at[i]

    here = pl.ds(pl.multiple_of(at.w * size, 8), size)
    going = exchange(piece(pk), mine(r1), NW, at.w, at.along_w, ss.at[0], rs.at[0])
    r1[at.w] = pk[here, :]
    yield
    finish(going)
    r2[at.z] = add_up(r1, NW)
    going = exchange(lambda _: r2.at[at.z], mine(r2), NZ, at.z, at.along_z, ss.at[1], rs.at[1])
    yield
    finish(going)
    total = add_up(r2, NZ)
    if over_snap:
        rx[at.x] = total
        going = exchange(lambda _: rx.at[at.x], mine(rx), NX, at.x, at.along_x, ss.at[2], rs.at[2])
        yield
        finish(going)
        total = add_up(rx, NX)
    out[here, :] = total
    going = exchange(lambda _: out.at[here], piece(out), NW, at.w, at.along_w, ss.at[3], rs.at[3])
    yield
    finish(going)


def run(steps):
    for _ in steps:
        pass


def pack(g, g_ref, pk, base):
    g_ref[:, : g.shape[1]] = g
    pk[base : base + 200, :] = g_ref[:, :128]
    pk[base + 200 : base + 272, :] = g_ref[128:200, 128:]


def unpack(pk, base, a_ref, b):
    a_ref[b, :, :128] = pk[base : base + 200, :]
    a_ref[b, 128:200, 128:] = pk[base + 200 : base + 272, :]
    a_ref[b, :128, 128:] = pk[base + 128 : base + 256, :].T


def main_kernel(
    x0_hbm, src_hbm, blk_hbm, cols_ref, sk_hbm, ms_hbm,
    zf_hbm, co_ref,
    zf_ref, x0_ref, src_ref, blk_ref, sk_ref, ms_ref, x1_ref, x2_ref, y_ref, dup_a, dup_b, out_h, in_h,
    yq, gs, u_ref, fac, tx, xr, ss_ref, d_ref,
    pk1, l1, l2, lo, pk2, p1, p2, px, po, pk3, c1, c2, co,
    in_sem, send_sem, recv_sem, s1, q1, s2, q2, s3, q3, sb, qb, st, qt,
):
    at = Where()
    x, c = at.x, at.c
    n = 200
    ncell = NZ * NW
    left, right = lax.rem(c + ncell - 1, ncell), lax.rem(c + 1, ncell)
    barrier = pltpu.get_barrier_semaphore()
    greeted = [(x, left), (x, right)]
    greeted += [at.along_z(lax.rem(at.z + d, NZ)) for d in range(1, NZ)]
    greeted += [at.along_w(lax.rem(at.w + d, NW)) for d in range(1, NW)]
    greeted += [at.along_x(lax.rem(at.x + d, NX)) for d in range(1, NX)]
    for device in greeted:
        pl.semaphore_signal(barrier, inc=1, device_id=device, device_id_type=MESH)
    moved = (
        (x0_hbm, x0_ref), (blk_hbm, blk_ref), (src_hbm.at[0], src_ref.at[0]), (src_hbm.at[1], src_ref.at[1]),
        (sk_hbm, sk_ref), (ms_hbm, ms_ref),
    )
    loads = [pltpu.make_async_copy(src, dst, in_sem.at[i]) for i, (src, dst) in enumerate(moved)]
    for ld in loads:
        ld.start()

    rows = x0_ref.shape[0]
    npair = x0_ref.shape[1] // 128
    low = lax.broadcasted_iota(jnp.int32, (rows, 128), 1) < 64

    def spread(tile, dup, p):
        turned = pltpu.roll(tile, 64, axis=1)
        dup[2 * p] = jnp.where(low, tile, turned).astype(BF16)
        dup[2 * p + 1] = jnp.where(low, turned, tile).astype(BF16)

    def lanes(p):
        return pl.ds(pl.multiple_of(p * 128, 128), 128)

    def copies(step):
        return [
            pltpu.make_async_remote_copy(
                src_ref=out_h.at[step, pl.ds(2 * side, 2)],
                dst_ref=in_h.at[step, pl.ds(2 - 2 * side, 2)],
                send_sem=send_sem.at[step, side],
                recv_sem=recv_sem.at[step, side],
                device_id=(x, peer),
                device_id_type=MESH,
            )
            for side, peer in ((0, left), (1, right))
        ]

    def apply(dup, xin, xout, s, p, then):
        sides = []
        for b2 in range(2):
            b = 2 * p + b2
            parts = []
            for jj in range(3):
                ca = cols_ref[2 * jj, b]
                cb = cols_ref[2 * jj + 1, b]
                parts.append(jnp.where(low, dup[ca], dup[cb]))
            parts.append(dup[cols_ref[6, b]][:, :64])
            picked = jnp.concatenate(parts, axis=1)
            sides.append(
                lax.dot_general(
                    picked, blk_ref[b], (((1,), (1,)), ((), ())), preferred_element_type=F32
                )
            )
        res = jnp.concatenate(sides, axis=1)
        new = xin[:, lanes(p)] - res + src_ref[s, :, lanes(p)].astype(F32)
        xout[:, lanes(p)] = new
        if then is not None:
            spread(new, then, p + 2)
        return new

    def arrive(step, dup):
        for e in range(2):
            spread(in_h[step, e].astype(F32), dup, e)
            spread(in_h[step, 2 + e].astype(F32), dup, npair + 2 + e)

    loads[0].wait()
    for e in range(2):
        out_h[0, e] = x0_ref[:, e * 128 : (e + 1) * 128].astype(BF16)
        q = npair - 2 + e
        out_h[0, 2 + e] = x0_ref[:, q * 128 : (q + 1) * 128].astype(BF16)
    pl.semaphore_wait(barrier, len(greeted))
    first = copies(0)
    for cp in first:
        cp.start()

    @pl.loop(0, npair)
    def _(p):
        spread(x0_ref[:, lanes(p)], dup_a, p + 2)

    loads[1].wait()
    loads[2].wait()

    @pl.loop(2, npair - 2)
    def _(p):
        apply(dup_a, x0_ref, x1_ref, 0, p, dup_b)

    for cp in first:
        cp.wait()
    arrive(0, dup_a)
    for e, p in enumerate((0, 1, npair - 2, npair - 1)):
        out_h[1, e] = apply(dup_a, x0_ref, x1_ref, 0, p, dup_b).astype(BF16)
    second = copies(1)
    for cp in second:
        cp.start()

    loads[3].wait()

    @pl.loop(2, npair - 2)
    def _(p):
        apply(dup_b, x1_ref, x2_ref, 1, p, None)

    for cp in second:
        cp.wait()
    arrive(1, dup_b)
    for p in (0, 1, npair - 2, npair - 1):
        apply(dup_b, x1_ref, x2_ref, 1, p, None)

    gs[...] = jnp.zeros_like(gs)
    loads[4].wait()
    gram = None
    for q in range(NX):
        cut = slice(q * 512, (q + 1) * 512)
        y_ref[q] = mm3(sk_ref[:, :rows], x1_ref[:, cut]) + mm3(sk_ref[:, rows:], x2_ref[:, cut])
        part = mm_nt(y_ref[q], y_ref[q])
        gram = part if gram is None else gram + part

    pk1[272:, :] = jnp.zeros((48, 128), F32)
    pack(gram, gs, pk1, 0)
    steps = reduce_steps(at, pk1, 40, (l1, l2, None, lo, s1, q1), False)
    next(steps)
    bulk = exchange(lambda peer: y_ref.at[peer], lambda i: yq.at[i], NX, x, at.along_x, sb.at[0], qb.at[0])
    yq[x] = y_ref[x]
    tx[:, :120, 128:] = jnp.zeros((NX, 120, 128), F32)
    pk2[888:, :] = jnp.zeros((8, 128), F32)
    pk3[...] = jnp.zeros_like(pk3)
    xr[...] = jnp.zeros_like(xr)
    d_ref[...] = jnp.zeros_like(d_ref)
    loads[5].wait()
    halves_of = [[ms_ref[level, :, n * h : n * h + n] for h in range(2)] for level in range(2)]
    ss_ref[...] = mm_nt(halves_of[1][0], halves_of[1][0]) + mm_nt(halves_of[1][1], halves_of[1][1])
    run(steps)
    unpack(lo, 0, fac, 0)
    shares = []

    def send_rows(k):
        part = (pl.ds(k * NB, NB), pl.ds(0, 128 if k < 3 else 256))
        shares.append(
            exchange(
                lambda _: fac.at[0, *part], lambda i: tx.at[i, *part], NX, x, at.along_x, st.at[k], qt.at[k]
            )
        )

    chol_inv(fac.at[pl.ds(0, 1)], 1, send_rows)
    tx[x] = fac[0]
    finish(bulk)
    for share in shares:
        finish(share)

    bulks = []
    for p in range(2):
        for h in range(2):
            u_ref[h, :, :n] = mm(halves_of[0][h], tx[2 * p + h][:, :n])
        m = mm(u_ref[0, :, :n], yq[2 * p]) + mm(u_ref[1, :, :n], yq[2 * p + 1])
        zf_ref[p, x] = m
        bulks.append(
            exchange(
                lambda _, p=p: zf_ref.at[p, x], lambda i, p=p: zf_ref.at[p, i],
                NX, x, at.along_x, sb.at[1 + p], qb.at[1 + p],
            )
        )
    for p in range(2):
        pack(mm_nt(zf_ref[p, x], zf_ref[p, x]), gs, pk2, 272 * p)
    pk2[544:744, :] = mm_nt(zf_ref[0, x], zf_ref[1, x, :128])
    xr[:, :n] = mm_nt(zf_ref[1, x, 128:], zf_ref[0, x])
    pk2[744:816, :] = xr[:, :128]
    pk2[816:888, :] = xr[:, 128:]
    steps = reduce_steps(at, pk2, 112, (p1, p2, px, po, s2, q2), True)
    next(steps)
    next(steps)
    for p in range(2):
        finish(bulks[p])
        raw = mm_nt(x2_ref[:, :512], zf_ref[p, 0])
        for q in range(1, NX):
            raw = raw + mm_nt(x2_ref[:, q * 512 : (q + 1) * 512], zf_ref[p, q])
        pk3[512 * p : 512 * p + 256, :] = raw[:, :128]
        pk3[512 * p + 256 : 512 * p + 512, :72] = raw[:, 128:]
        next(steps)
    keep = pltpu.make_async_copy(zf_ref, zf_hbm, in_sem.at[6])
    keep.start()
    last = reduce_steps(at, pk3, 128, (c1, c2, None, co, s3, q3), False)
    next(last)
    run(steps)

    for p in range(2):
        unpack(po, 272 * p, fac, p)
    gs[:, :128] = po[544:744, :]
    xr[:, :128] = po[744:816, :]
    xr[:, 128:] = po[816:888, :]
    gs[:, 128:n] = xr[...].T[:n]

    def go_on(k):
        if k == 1:
            next(last)

    chol_inv(fac, 2, go_on)
    for p in range(2):
        u_ref[p, :, :n] = mm(halves_of[1][p], fac[p][:, :n])
    d_ref[:, :n] = mm_nt(mm(u_ref[0, :, :n], gs[:, :n]), u_ref[1, :, :n])
    fac[0, :, :n] = ss_ref[...] + d_ref[:, :n] + d_ref[...].T[:n, :n]
    chol_inv(fac.at[pl.ds(0, 1)], 1, go_on)
    for p in range(2):
        u_ref[p, :, :n] = mm(fac[0][:, :n], u_ref[p, :, :n])
    run(last)
    inner = None
    for p in range(2):
        base = 512 * p
        part = mm_nt(co[base : base + 256, :], u_ref[p, :, :128])
        part = part + mm_nt(co[base + 256 : base + 512, :][:, :72], u_ref[p, :, 128:n])
        inner = part if inner is None else inner + part
    for p in range(2):
        co_ref[p] = mm(inner, u_ref[p, :, :n])
    keep.wait()


def merged_top(start_states, sources, blocks, cols, leaf_sketch, merge_sketch):
    rows, width = start_states.shape
    rank = leaf_sketch.shape[0]
    part = width // NX
    nblk = width // 64
    anywhere = pl.BlockSpec(memory_space=pl.ANY)
    vmem = pl.BlockSpec(memory_space=pltpu.VMEM)
    dma = pltpu.SemaphoreType.DMA

    def buf(*shape, dtype=F32):
        return pltpu.VMEM(shape, dtype)

    return pl.pallas_call(
        main_kernel,
        name="merged_top",
        out_shape=(
            jax.ShapeDtypeStruct((2, NX, rank, part), F32),
            jax.ShapeDtypeStruct((2, rows, rank), F32),
        ),
        in_specs=[anywhere] * 3 + [pl.BlockSpec(memory_space=pltpu.SMEM)] + [anywhere] * 2,
        out_specs=(anywhere, vmem),
        scratch_shapes=[
            buf(2, NX, rank, part), buf(rows, width), buf(*sources.shape, dtype=BF16), buf(*blocks.shape, dtype=BF16),
            buf(*leaf_sketch.shape), buf(*merge_sketch.shape),
            buf(rows, width), buf(rows, width), buf(NX, rank, part),
            buf(nblk + 2 * HB, rows, 128, dtype=BF16), buf(nblk + 2 * HB, rows, 128, dtype=BF16),
            buf(2, 4, rows, 128, dtype=BF16), buf(2, 4, rows, 128, dtype=BF16),
            buf(NX, rank, part), buf(rank, 256), buf(2, rank, 256), buf(2, rank, 256), buf(NX, rank, 256),
            buf(72, 256), buf(rank, rank), buf(rank, 256),
            buf(320, 128), buf(NW, 40, 128), buf(NZ, 40, 128), buf(320, 128),
            buf(896, 128), buf(NW, 112, 128), buf(NZ, 112, 128), buf(NX, 112, 128), buf(896, 128),
            buf(1024, 128), buf(NW, 128, 128), buf(NZ, 128, 128), buf(1024, 128),
            dma((7,)), dma((2, 2)), dma((2, 2)),
            dma((4, 8)), dma((4, 8)), dma((4, 8)), dma((4, 8)), dma((4, 8)), dma((4, 8)),
            dma((3, 4)), dma((3, 4)), dma((5, 4)), dma((5, 4)),
        ],
        compiler_params=pltpu.CompilerParams(
            collective_id=0, has_side_effects=True, vmem_limit_bytes=60 * 2**20
        ),
    )(start_states, sources, blocks, cols, leaf_sketch, merge_sketch)


def project_kernel(co_ref, z_ref, o_ref):
    o_ref[...] = mm3(co_ref[0], z_ref[0, 0]) + mm3(co_ref[1], z_ref[1, 0])


def project(coeffs, z):
    _, rows, rank = coeffs.shape
    parts, part = z.shape[1], z.shape[3]
    return pl.pallas_call(
        project_kernel,
        name="project",
        grid=(parts,),
        out_shape=jax.ShapeDtypeStruct((rows, parts * part), F32),
        in_specs=[
            pl.BlockSpec((2, rows, rank), lambda q: (0, 0, 0)),
            pl.BlockSpec((2, 1, rank, part), lambda q: (0, q, 0, 0)),
        ],
        out_specs=pl.BlockSpec((rows, part), lambda q: (0, q)),
        compiler_params=pltpu.CompilerParams(vmem_limit_bytes=60 * 2**20),
    )(coeffs, z)


def local(start_states, sources, blocks, columns, leaf_sketch, merge_sketch):
    cols = columns.T - lax.axis_index("cell") * blocks.shape[0] + HB
    z, coeffs = merged_top(start_states, sources, blocks, cols, leaf_sketch, merge_sketch)
    return project(coeffs, z)


def solution(mesh):
    placed = (
        P("snap", "cell"),
        P(None, "snap", "cell"),
        P("cell", None, None),
        P("cell", None),
        P(),
        P(),
    )
    return jax.shard_map(
        local, mesh=mesh, in_specs=placed, out_specs=P("snap", "cell"), check_vma=False
    )
```

```python
import jax
import jax.numpy as jnp
from jax import lax
from jax.experimental import pallas as pl
from jax.experimental.pallas import tpu as pltpu
from jax.sharding import PartitionSpec as P

HB = 4
NZ = 8
NW = 8
NX = 4
NB = 40
MESH = pl.DeviceIdType.MESH
F32 = jnp.float32
BF16 = jnp.bfloat16


def mm(a, b):
    return jnp.dot(a, b, precision=lax.Precision.HIGHEST, preferred_element_type=F32)


def halves(a):
    high = a.astype(BF16)
    return high, (a - high.astype(F32)).astype(BF16)


def mm3(a, b):
    ah, al = halves(a)
    bh, bl = halves(b)
    small = jnp.dot(ah, bl, preferred_element_type=F32) + jnp.dot(al, bh, preferred_element_type=F32)
    return jnp.dot(ah, bh, preferred_element_type=F32) + small


def mm_nt(a, b):
    return lax.dot_general(
        a, b, (((1,), (1,)), ((), ())), precision=lax.Precision.HIGHEST, preferred_element_type=F32
    )


def eliminate(tiles):
    nt = len(tiles[0])
    sub = lax.broadcasted_iota(jnp.int32, (8, 128), 0)
    for t in range(nt):
        cols = [
            [
                [jnp.broadcast_to(r[u][:, 8 * t + j : 8 * t + j + 1], (8, 128)) for j in range(8)]
                for u in range(t, nt)
            ]
            for r in tiles
        ]
        for j in range(8):
            for r, cl in zip(tiles, cols):
                pivot = jnp.broadcast_to(cl[0][j][j : j + 1], (8, 128))
                inv = lax.rsqrt(pivot)
                row = jnp.broadcast_to(r[t][j : j + 1], (8, 128)) * inv
                heads = [jnp.broadcast_to(cl[0][j][m : m + 1], (8, 128)) * inv for m in range(j + 1, 8)]
                for u in range(t, nt):
                    lcol = cl[u - t][j] * inv
                    if u == t:
                        lcol = jnp.where(sub > j, lcol, 0.0)
                        r[u] = jnp.where(sub == j, row, r[u] - lcol * row)
                    else:
                        r[u] = r[u] - lcol * row
                    for m in range(j + 1, 8):
                        cl[u - t][m] = cl[u - t][m] - lcol * heads[m - j - 1]
    return tiles


def chol_inv(a_ref, batch, after=None):
    n = a_ref.shape[1]
    lane = lax.broadcasted_iota(jnp.int32, (NB, 128), 1)
    srow = lax.broadcasted_iota(jnp.int32, (NB, 128), 0)
    lane2 = lax.broadcasted_iota(jnp.int32, (NB, 256), 1)
    srow2 = lax.broadcasted_iota(jnp.int32, (NB, 256), 0)
    for k in range(n // NB):
        lo = k * NB
        hi = lo + NB
        tiles = []
        for b in range(batch):
            blk = a_ref[b, lo:hi, :]
            if lo:
                blk = pltpu.roll(blk, 256 - lo, axis=1)
            blk = jnp.where(lane < NB, blk[:, :128], jnp.where(lane == 64 + srow, 1.0, 0.0))
            tiles.append([blk[8 * t : 8 * t + 8] for t in range(NB // 8)])
        tiles = eliminate(tiles)
        for b in range(batch):
            tk = pltpu.roll(jnp.concatenate(tiles[b], axis=0), 64, axis=1)[:, :NB]
            own = jnp.where(lane2 - lo == srow2, 1.0, 0.0)
            w = mm(tk, jnp.where((lane2 >= lo) & (lane2 < hi), own, a_ref[b, lo:hi, :]))
            if hi < n:
                lane3 = lax.broadcasted_iota(jnp.int32, (n - hi, 256), 1)
                rest = jnp.where((lane3 >= lo) & (lane3 < hi), 0.0, a_ref[b, hi:, :])
                a_ref[b, hi:, :] = rest - mm(w.T[hi:n], w)
            a_ref[b, lo:hi, :] = jnp.where(lane2 < hi, w, 0.0)
        if after is not None:
            after(k)


def exchange(src_of, dst_of, count, me, device_of, send_sem, recv_sem):
    sends, waits = [], []
    for d in range(1, count):
        peer = lax.rem(me + d, count)
        origin = lax.rem(me + count - d, count)

        def copy(slot, peer=peer, d=d):
            return pltpu.make_async_remote_copy(
                src_ref=src_of(peer), dst_ref=dst_of(slot), send_sem=send_sem.at[d], recv_sem=recv_sem.at[slot],
                device_id=device_of(peer), device_id_type=MESH,
            )

        cp = copy(me)
        cp.start()
        sends.append(cp)
        waits.append(copy(origin))
    return sends, waits


def finish(pair):
    sends, waits = pair
    for w in waits:
        w.wait_recv()
    for s in sends:
        s.wait_send()


def add_up(ref, count):
    total = ref[0]
    for i in range(1, count):
        total = total + ref[i]
    return total


class Where:
    def __init__(self):
        self.x = lax.axis_index("snap")
        self.c = lax.axis_index("cell")
        self.z, self.w = self.c // NW, lax.rem(self.c, NW)

    def along_z(self, peer):
        return (self.x, peer * NW + self.w)

    def along_w(self, peer):
        return (self.x, self.z * NW + peer)

    def along_x(self, peer):
        return (peer, self.z * NW + self.w)


def reduce_steps(at, pk, size, bufs, over_snap):
    r1, r2, rx, out, ss, rs = bufs

    def piece(ref):
        return lambda i: ref.at[pl.ds(pl.multiple_of(i * size, 8), size)]

    def mine(ref):
        return lambda i: ref.at[i]

    here = pl.ds(pl.multiple_of(at.w * size, 8), size)
    going = exchange(piece(pk), mine(r1), NW, at.w, at.along_w, ss.at[0], rs.at[0])
    r1[at.w] = pk[here, :]
    yield
    finish(going)
    r2[at.z] = add_up(r1, NW)
    going = exchange(lambda _: r2.at[at.z], mine(r2), NZ, at.z, at.along_z, ss.at[1], rs.at[1])
    yield
    finish(going)
    total = add_up(r2, NZ)
    if over_snap:
        rx[at.x] = total
        going = exchange(lambda _: rx.at[at.x], mine(rx), NX, at.x, at.along_x, ss.at[2], rs.at[2])
        yield
        finish(going)
        total = add_up(rx, NX)
    out[here, :] = total
    going = exchange(lambda _: out.at[here], piece(out), NW, at.w, at.along_w, ss.at[3], rs.at[3])
    yield
    finish(going)


def run(steps):
    for _ in steps:
        pass


def pack(g, g_ref, pk, base):
    g_ref[:, : g.shape[1]] = g
    pk[base : base + 200, :] = g_ref[:, :128]
    pk[base + 200 : base + 272, :] = g_ref[128:200, 128:]


def unpack(pk, base, a_ref, b):
    a_ref[b, :, :128] = pk[base : base + 200, :]
    a_ref[b, 128:200, 128:] = pk[base + 200 : base + 272, :]
    a_ref[b, :128, 128:] = pk[base + 128 : base + 256, :].T


def main_kernel(
    x0_hbm, src_hbm, blk_hbm, cols_ref, sk_hbm, ms_hbm,
    zf_hbm, co_ref,
    zf_ref, x0_ref, src_ref, blk_ref, sk_ref, ms_ref, x1_ref, x2_ref, y_ref, dup_a, dup_b, out_h, in_h,
    yq, gs, u_ref, fac, tx, xr, ss_ref, d_ref,
    pk1, l1, l2, lo, pk2, p1, p2, px, po, pk3, c1, c2, co, pk4, e1, e2, eo,
    in_sem, send_sem, recv_sem, s1, q1, s2, q2, s3, q3, s4, q4, sb, qb, st, qt,
):
    at = Where()
    x, c = at.x, at.c
    n = 200
    ncell = NZ * NW
    left, right = lax.rem(c + ncell - 1, ncell), lax.rem(c + 1, ncell)
    barrier = pltpu.get_barrier_semaphore()
    greeted = [(x, left), (x, right)]
    greeted += [at.along_z(lax.rem(at.z + d, NZ)) for d in range(1, NZ)]
    greeted += [at.along_w(lax.rem(at.w + d, NW)) for d in range(1, NW)]
    greeted += [at.along_x(lax.rem(at.x + d, NX)) for d in range(1, NX)]
    for device in greeted:
        pl.semaphore_signal(barrier, inc=1, device_id=device, device_id_type=MESH)
    moved = (
        (x0_hbm, x0_ref), (blk_hbm, blk_ref), (src_hbm.at[0], src_ref.at[0]), (src_hbm.at[1], src_ref.at[1]),
        (sk_hbm, sk_ref), (ms_hbm, ms_ref),
    )
    loads = [pltpu.make_async_copy(src, dst, in_sem.at[i]) for i, (src, dst) in enumerate(moved)]
    for ld in loads:
        ld.start()

    rows = x0_ref.shape[0]
    npair = x0_ref.shape[1] // 128
    low = lax.broadcasted_iota(jnp.int32, (rows, 128), 1) < 64

    def spread(tile, dup, p):
        turned = pltpu.roll(tile, 64, axis=1)
        dup[2 * p] = jnp.where(low, tile, turned).astype(BF16)
        dup[2 * p + 1] = jnp.where(low, turned, tile).astype(BF16)

    def lanes(p):
        return pl.ds(pl.multiple_of(p * 128, 128), 128)

    def copies(step):
        return [
            pltpu.make_async_remote_copy(
                src_ref=out_h.at[step, pl.ds(2 * side, 2)],
                dst_ref=in_h.at[step, pl.ds(2 - 2 * side, 2)],
                send_sem=send_sem.at[step, side],
                recv_sem=recv_sem.at[step, side],
                device_id=(x, peer),
                device_id_type=MESH,
            )
            for side, peer in ((0, left), (1, right))
        ]

    def apply(dup, xin, xout, s, p, then):
        sides = []
        for b2 in range(2):
            b = 2 * p + b2
            parts = []
            for jj in range(3):
                ca = cols_ref[2 * jj, b]
                cb = cols_ref[2 * jj + 1, b]
                parts.append(jnp.where(low, dup[ca], dup[cb]))
            parts.append(dup[cols_ref[6, b]][:, :64])
            picked = jnp.concatenate(parts, axis=1)
            sides.append(
                lax.dot_general(
                    picked, blk_ref[b], (((1,), (1,)), ((), ())), preferred_element_type=F32
                )
            )
        res = jnp.concatenate(sides, axis=1)
        new = xin[:, lanes(p)] - res + src_ref[s, :, lanes(p)].astype(F32)
        xout[:, lanes(p)] = new
        if then is not None:
            spread(new, then, p + 2)
        return new

    def arrive(step, dup):
        for e in range(2):
            spread(in_h[step, e].astype(F32), dup, e)
            spread(in_h[step, 2 + e].astype(F32), dup, npair + 2 + e)

    loads[0].wait()
    for e in range(2):
        out_h[0, e] = x0_ref[:, e * 128 : (e + 1) * 128].astype(BF16)
        q = npair - 2 + e
        out_h[0, 2 + e] = x0_ref[:, q * 128 : (q + 1) * 128].astype(BF16)
    pl.semaphore_wait(barrier, len(greeted))
    first = copies(0)
    for cp in first:
        cp.start()

    @pl.loop(0, npair)
    def _(p):
        spread(x0_ref[:, lanes(p)], dup_a, p + 2)

    loads[1].wait()
    loads[2].wait()

    @pl.loop(2, npair - 2)
    def _(p):
        apply(dup_a, x0_ref, x1_ref, 0, p, dup_b)

    for cp in first:
        cp.wait()
    arrive(0, dup_a)
    for e, p in enumerate((0, 1, npair - 2, npair - 1)):
        out_h[1, e] = apply(dup_a, x0_ref, x1_ref, 0, p, dup_b).astype(BF16)
    second = copies(1)
    for cp in second:
        cp.start()

    loads[3].wait()

    @pl.loop(2, npair - 2)
    def _(p):
        apply(dup_b, x1_ref, x2_ref, 1, p, None)

    for cp in second:
        cp.wait()
    arrive(1, dup_b)
    for p in (0, 1, npair - 2, npair - 1):
        apply(dup_b, x1_ref, x2_ref, 1, p, None)

    gs[...] = jnp.zeros_like(gs)
    loads[4].wait()
    gram = None
    for q in range(NX):
        cut = slice(q * 512, (q + 1) * 512)
        y_ref[q] = mm3(sk_ref[:, :rows], x1_ref[:, cut]) + mm3(sk_ref[:, rows:], x2_ref[:, cut])
        part = mm_nt(y_ref[q], y_ref[q])
        gram = part if gram is None else gram + part

    pk1[272:, :] = jnp.zeros((48, 128), F32)
    pack(gram, gs, pk1, 0)
    steps = reduce_steps(at, pk1, 40, (l1, l2, None, lo, s1, q1), False)
    next(steps)
    bulk = exchange(lambda peer: y_ref.at[peer], lambda i: yq.at[i], NX, x, at.along_x, sb.at[0], qb.at[0])
    yq[x] = y_ref[x]
    tx[:, :120, 128:] = jnp.zeros((NX, 120, 128), F32)
    pk2[888:, :] = jnp.zeros((8, 128), F32)
    pk3[...] = jnp.zeros_like(pk3)
    pk4[...] = jnp.zeros_like(pk4)
    xr[...] = jnp.zeros_like(xr)
    d_ref[...] = jnp.zeros_like(d_ref)
    loads[5].wait()
    halves_of = [[ms_ref[level, :, n * h : n * h + n] for h in range(2)] for level in range(2)]
    ss_ref[...] = mm_nt(halves_of[1][0], halves_of[1][0]) + mm_nt(halves_of[1][1], halves_of[1][1])
    run(steps)
    unpack(lo, 0, fac, 0)
    shares = []

    def send_rows(k):
        part = (pl.ds(k * NB, NB), pl.ds(0, 128 if k < 3 else 256))
        shares.append(
            exchange(
                lambda _: fac.at[0, *part], lambda i: tx.at[i, *part], NX, x, at.along_x, st.at[k], qt.at[k]
            )
        )

    chol_inv(fac.at[pl.ds(0, 1)], 1, send_rows)
    tx[x] = fac[0]
    finish(bulk)
    for share in shares:
        finish(share)

    def send_pair(p, lo, hi, lane):
        return exchange(
            lambda _: zf_ref.at[p, x, lo:hi], lambda i: zf_ref.at[p, i, lo:hi],
            NX, x, at.along_x, sb.at[lane], qb.at[lane],
        )

    def inner_products(p, pk):
        raw = mm_nt(x2_ref[:, :512], zf_ref[p, 0])
        for q in range(1, NX):
            raw = raw + mm_nt(x2_ref[:, q * 512 : (q + 1) * 512], zf_ref[p, q])
        pk[:rows, :] = raw[:, :128]
        pk[rows:, :72] = raw[:, 128:]

    bulks = []
    for p in range(2):
        for h in range(2):
            u_ref[h, :, :n] = mm(halves_of[0][h], tx[2 * p + h][:, :n])
        zf_ref[p, x] = mm(u_ref[0, :, :n], yq[2 * p]) + mm(u_ref[1, :, :n], yq[2 * p + 1])
        bulks.append(send_pair(p, 0, (n, 56)[p], 1 + p))
    for p in range(2):
        pack(mm_nt(zf_ref[p, x], zf_ref[p, x]), gs, pk2, 272 * p)
    pk2[544:744, :] = mm_nt(zf_ref[0, x], zf_ref[1, x, :128])
    xr[:, :n] = mm_nt(zf_ref[1, x, 128:], zf_ref[0, x])
    pk2[744:816, :] = xr[:, :128]
    pk2[816:888, :] = xr[:, 128:]
    products = reduce_steps(at, pk2, 112, (p1, p2, px, po, s2, q2), True)
    first = reduce_steps(at, pk3, 64, (c1, c2, None, co, s3, q3), False)
    second = reduce_steps(at, pk4, 64, (e1, e2, None, eo, s4, q4), False)
    next(products)
    next(products)
    finish(bulks[0])
    inner_products(0, pk3)
    next(first)
    next(products)
    bulks.append(send_pair(1, 56, n, 3))
    next(first)
    next(products)
    run(products)
    next(first)

    for p in range(2):
        unpack(po, 272 * p, fac, p)
    gs[:, :128] = po[544:744, :]
    xr[:, :128] = po[744:816, :]
    xr[:, 128:] = po[816:888, :]
    gs[:, 128:n] = xr[...].T[:n]
    keep = pltpu.make_async_copy(zf_ref, zf_hbm, in_sem.at[6])

    def during_pairs(k):
        if k == 1:
            finish(bulks[1])
            finish(bulks[2])
            keep.start()
            inner_products(1, pk4)
            next(second)
        if k == 4:
            next(second)

    def during_top(k):
        if k == 2:
            next(second)

    chol_inv(fac, 2, during_pairs)
    run(first)
    for p in range(2):
        u_ref[p, :, :n] = mm(halves_of[1][p], fac[p][:, :n])
    d_ref[:, :n] = mm_nt(mm(u_ref[0, :, :n], gs[:, :n]), u_ref[1, :, :n])
    fac[0, :, :n] = ss_ref[...] + d_ref[:, :n] + d_ref[...].T[:n, :n]
    chol_inv(fac.at[pl.ds(0, 1)], 1, during_top)
    for p in range(2):
        u_ref[p, :, :n] = mm(fac[0][:, :n], u_ref[p, :, :n])

    def in_top(p, total):
        return mm_nt(total[:rows, :], u_ref[p, :, :128]) + mm_nt(total[rows:, :][:, :72], u_ref[p, :, 128:n])

    inner = in_top(0, co)
    run(second)
    inner = inner + in_top(1, eo)
    for p in range(2):
        co_ref[p] = mm(inner, u_ref[p, :, :n])
    keep.wait()


def merged_top(start_states, sources, blocks, cols, leaf_sketch, merge_sketch):
    rows, width = start_states.shape
    rank = leaf_sketch.shape[0]
    part = width // NX
    nblk = width // 64
    anywhere = pl.BlockSpec(memory_space=pl.ANY)
    vmem = pl.BlockSpec(memory_space=pltpu.VMEM)
    dma = pltpu.SemaphoreType.DMA

    def buf(*shape, dtype=F32):
        return pltpu.VMEM(shape, dtype)

    return pl.pallas_call(
        main_kernel,
        name="merged_top",
        out_shape=(
            jax.ShapeDtypeStruct((2, NX, rank, part), F32),
            jax.ShapeDtypeStruct((2, rows, rank), F32),
        ),
        in_specs=[anywhere] * 3 + [pl.BlockSpec(memory_space=pltpu.SMEM)] + [anywhere] * 2,
        out_specs=(anywhere, vmem),
        scratch_shapes=[
            buf(2, NX, rank, part), buf(rows, width), buf(*sources.shape, dtype=BF16), buf(*blocks.shape, dtype=BF16),
            buf(*leaf_sketch.shape), buf(*merge_sketch.shape),
            buf(rows, width), buf(rows, width), buf(NX, rank, part),
            buf(nblk + 2 * HB, rows, 128, dtype=BF16), buf(nblk + 2 * HB, rows, 128, dtype=BF16),
            buf(2, 4, rows, 128, dtype=BF16), buf(2, 4, rows, 128, dtype=BF16),
            buf(NX, rank, part), buf(rank, 256), buf(2, rank, 256), buf(2, rank, 256), buf(NX, rank, 256),
            buf(72, 256), buf(rank, rank), buf(rank, 256),
            buf(320, 128), buf(NW, 40, 128), buf(NZ, 40, 128), buf(320, 128),
            buf(896, 128), buf(NW, 112, 128), buf(NZ, 112, 128), buf(NX, 112, 128), buf(896, 128),
            buf(512, 128), buf(NW, 64, 128), buf(NZ, 64, 128), buf(512, 128),
            buf(512, 128), buf(NW, 64, 128), buf(NZ, 64, 128), buf(512, 128),
            dma((7,)), dma((2, 2)), dma((2, 2)),
            dma((4, 8)), dma((4, 8)), dma((4, 8)), dma((4, 8)), dma((4, 8)), dma((4, 8)), dma((4, 8)), dma((4, 8)),
            dma((4, 4)), dma((4, 4)), dma((5, 4)), dma((5, 4)),
        ],
        compiler_params=pltpu.CompilerParams(
            collective_id=0, has_side_effects=True, vmem_limit_bytes=60 * 2**20
        ),
    )(start_states, sources, blocks, cols, leaf_sketch, merge_sketch)


def project_kernel(co_ref, z_ref, o_ref):
    o_ref[...] = mm3(co_ref[0], z_ref[0, 0]) + mm3(co_ref[1], z_ref[1, 0])


def project(coeffs, z):
    _, rows, rank = coeffs.shape
    parts, part = z.shape[1], z.shape[3]
    return pl.pallas_call(
        project_kernel,
        name="project",
        grid=(parts,),
        out_shape=jax.ShapeDtypeStruct((rows, parts * part), F32),
        in_specs=[
            pl.BlockSpec((2, rows, rank), lambda q: (0, 0, 0)),
            pl.BlockSpec((2, 1, rank, part), lambda q: (0, q, 0, 0)),
        ],
        out_specs=pl.BlockSpec((rows, part), lambda q: (0, q)),
        compiler_params=pltpu.CompilerParams(vmem_limit_bytes=60 * 2**20),
    )(coeffs, z)


def local(start_states, sources, blocks, columns, leaf_sketch, merge_sketch):
    cols = columns.T - lax.axis_index("cell") * blocks.shape[0] + HB
    z, coeffs = merged_top(start_states, sources, blocks, cols, leaf_sketch, merge_sketch)
    return project(coeffs, z)


def solution(mesh):
    placed = (
        P("snap", "cell"),
        P(None, "snap", "cell"),
        P("cell", None, None),
        P("cell", None),
        P(),
        P(),
    )
    return jax.shard_map(
        local, mesh=mesh, in_specs=placed, out_specs=P("snap", "cell"), check_vma=False
    )
```

```python
import jax
import jax.numpy as jnp
from jax import lax
from jax.experimental import pallas as pl
from jax.experimental.pallas import tpu as pltpu
from jax.sharding import PartitionSpec as P

HB = 4
NZ = 8
NW = 8
NX = 4
NB = 40
MESH = pl.DeviceIdType.MESH
F32 = jnp.float32
BF16 = jnp.bfloat16


def mm(a, b):
    return jnp.dot(a, b, precision=lax.Precision.HIGHEST, preferred_element_type=F32)


def halves(a):
    high = a.astype(BF16)
    return high, (a - high.astype(F32)).astype(BF16)


def mm3(a, b):
    ah, al = halves(a)
    bh, bl = halves(b)
    small = jnp.dot(ah, bl, preferred_element_type=F32) + jnp.dot(al, bh, preferred_element_type=F32)
    return jnp.dot(ah, bh, preferred_element_type=F32) + small


def mm3_nt(a, b):
    def dot(u, v):
        return lax.dot_general(u, v, (((1,), (1,)), ((), ())), preferred_element_type=F32)

    ah, al = halves(a)
    bh, bl = halves(b)
    return dot(ah, bh) + (dot(ah, bl) + dot(al, bh))


def mm_nt(a, b):
    return lax.dot_general(
        a, b, (((1,), (1,)), ((), ())), precision=lax.Precision.HIGHEST, preferred_element_type=F32
    )


def eliminate(tiles):
    nt = len(tiles[0])
    sub = lax.broadcasted_iota(jnp.int32, (8, 128), 0)
    for t in range(nt):
        cols = [
            [
                [jnp.broadcast_to(r[u][:, 8 * t + j : 8 * t + j + 1], (8, 128)) for j in range(8)]
                for u in range(t, nt)
            ]
            for r in tiles
        ]
        for j in range(8):
            for r, cl in zip(tiles, cols):
                pivot = jnp.broadcast_to(cl[0][j][j : j + 1], (8, 128))
                inv = lax.rsqrt(pivot)
                row = jnp.broadcast_to(r[t][j : j + 1], (8, 128)) * inv
                heads = [jnp.broadcast_to(cl[0][j][m : m + 1], (8, 128)) * inv for m in range(j + 1, 8)]
                for u in range(t, nt):
                    lcol = cl[u - t][j] * inv
                    if u == t:
                        lcol = jnp.where(sub > j, lcol, 0.0)
                        r[u] = jnp.where(sub == j, row, r[u] - lcol * row)
                    else:
                        r[u] = r[u] - lcol * row
                    for m in range(j + 1, 8):
                        cl[u - t][m] = cl[u - t][m] - lcol * heads[m - j - 1]
    return tiles


def chol_inv(a_ref, batch, after=None):
    n = a_ref.shape[1]
    lane = lax.broadcasted_iota(jnp.int32, (NB, 128), 1)
    srow = lax.broadcasted_iota(jnp.int32, (NB, 128), 0)
    lane2 = lax.broadcasted_iota(jnp.int32, (NB, 256), 1)
    srow2 = lax.broadcasted_iota(jnp.int32, (NB, 256), 0)
    for k in range(n // NB):
        lo = k * NB
        hi = lo + NB
        tiles = []
        for b in range(batch):
            blk = a_ref[b, lo:hi, :]
            if lo:
                blk = pltpu.roll(blk, 256 - lo, axis=1)
            blk = jnp.where(lane < NB, blk[:, :128], jnp.where(lane == 64 + srow, 1.0, 0.0))
            tiles.append([blk[8 * t : 8 * t + 8] for t in range(NB // 8)])
        tiles = eliminate(tiles)
        for b in range(batch):
            tk = pltpu.roll(jnp.concatenate(tiles[b], axis=0), 64, axis=1)[:, :NB]
            own = jnp.where(lane2 - lo == srow2, 1.0, 0.0)
            w = mm(tk, jnp.where((lane2 >= lo) & (lane2 < hi), own, a_ref[b, lo:hi, :]))
            if hi < n:
                lane3 = lax.broadcasted_iota(jnp.int32, (n - hi, 256), 1)
                rest = jnp.where((lane3 >= lo) & (lane3 < hi), 0.0, a_ref[b, hi:, :])
                a_ref[b, hi:, :] = rest - mm(w.T[hi:n], w)
            a_ref[b, lo:hi, :] = jnp.where(lane2 < hi, w, 0.0)
        if after is not None:
            after(k)


def exchange(src_of, dst_of, count, me, device_of, send_sem, recv_sem):
    sends, waits = [], []
    for d in range(1, count):
        peer = lax.rem(me + d, count)
        origin = lax.rem(me + count - d, count)

        def copy(slot, peer=peer, d=d):
            return pltpu.make_async_remote_copy(
                src_ref=src_of(peer), dst_ref=dst_of(slot), send_sem=send_sem.at[d], recv_sem=recv_sem.at[slot],
                device_id=device_of(peer), device_id_type=MESH,
            )

        cp = copy(me)
        cp.start()
        sends.append(cp)
        waits.append(copy(origin))
    return sends, waits


def finish(pair):
    sends, waits = pair
    for w in waits:
        w.wait_recv()
    for s in sends:
        s.wait_send()


def add_up(ref, count):
    total = ref[0]
    for i in range(1, count):
        total = total + ref[i]
    return total


class Where:
    def __init__(self):
        self.x = lax.axis_index("snap")
        self.c = lax.axis_index("cell")
        self.z, self.w = self.c // NW, lax.rem(self.c, NW)

    def along_z(self, peer):
        return (self.x, peer * NW + self.w)

    def along_w(self, peer):
        return (self.x, self.z * NW + peer)

    def along_x(self, peer):
        return (peer, self.z * NW + self.w)


def reduce_steps(at, pk, size, bufs, over_snap):
    r1, r2, rx, out, ss, rs = bufs

    def piece(ref):
        return lambda i: ref.at[pl.ds(pl.multiple_of(i * size, 8), size)]

    def mine(ref):
        return lambda i: ref.at[i]

    here = pl.ds(pl.multiple_of(at.w * size, 8), size)
    going = exchange(piece(pk), mine(r1), NW, at.w, at.along_w, ss.at[0], rs.at[0])
    r1[at.w] = pk[here, :]
    yield
    finish(going)
    r2[at.z] = add_up(r1, NW)
    going = exchange(lambda _: r2.at[at.z], mine(r2), NZ, at.z, at.along_z, ss.at[1], rs.at[1])
    yield
    finish(going)
    total = add_up(r2, NZ)
    if over_snap:
        rx[at.x] = total
        going = exchange(lambda _: rx.at[at.x], mine(rx), NX, at.x, at.along_x, ss.at[2], rs.at[2])
        yield
        finish(going)
        total = add_up(rx, NX)
    out[here, :] = total
    going = exchange(lambda _: out.at[here], piece(out), NW, at.w, at.along_w, ss.at[3], rs.at[3])
    yield
    finish(going)


def run(steps):
    for _ in steps:
        pass


def pack(g, g_ref, pk, base):
    g_ref[:, : g.shape[1]] = g
    pk[base : base + 200, :] = g_ref[:, :128]
    pk[base + 200 : base + 272, :] = g_ref[128:200, 128:]


def unpack(pk, base, a_ref, b):
    a_ref[b, :, :128] = pk[base : base + 200, :]
    a_ref[b, 128:200, 128:] = pk[base + 200 : base + 272, :]
    a_ref[b, :128, 128:] = pk[base + 128 : base + 256, :].T


def main_kernel(
    x0_hbm, src_hbm, blk_hbm, cols_ref, sk_hbm, ms_hbm,
    zf_hbm, co_ref,
    zf_ref, x0_ref, src_ref, blk_ref, sk_ref, ms_ref, x1_ref, x2_ref, y_ref, dup_a, dup_b, out_h, in_h,
    yq, gs, u_ref, fac, tx, xr, ss_ref, d_ref,
    pk1, l1, l2, lo, pk2, p1, p2, px, po, pk3, c1, c2, co, pk4, e1, e2, eo, pk5, r1, r2, rx, ro,
    in_sem, send_sem, recv_sem, s1, q1, s2, q2, s3, q3, s4, q4, s5, q5, sb, qb, st, qt,
):
    at = Where()
    x, c = at.x, at.c
    n = 200
    ncell = NZ * NW
    left, right = lax.rem(c + ncell - 1, ncell), lax.rem(c + 1, ncell)
    barrier = pltpu.get_barrier_semaphore()
    greeted = [(x, left), (x, right)]
    greeted += [at.along_z(lax.rem(at.z + d, NZ)) for d in range(1, NZ)]
    greeted += [at.along_w(lax.rem(at.w + d, NW)) for d in range(1, NW)]
    greeted += [at.along_x(lax.rem(at.x + d, NX)) for d in range(1, NX)]
    for device in greeted:
        pl.semaphore_signal(barrier, inc=1, device_id=device, device_id_type=MESH)
    moved = (
        (x0_hbm, x0_ref), (blk_hbm, blk_ref), (src_hbm.at[0], src_ref.at[0]), (src_hbm.at[1], src_ref.at[1]),
        (sk_hbm, sk_ref), (ms_hbm, ms_ref),
    )
    loads = [pltpu.make_async_copy(src, dst, in_sem.at[i]) for i, (src, dst) in enumerate(moved)]
    for ld in loads:
        ld.start()

    rows = x0_ref.shape[0]
    npair = x0_ref.shape[1] // 128
    low = lax.broadcasted_iota(jnp.int32, (rows, 128), 1) < 64

    def spread(tile, dup, p):
        turned = pltpu.roll(tile, 64, axis=1)
        dup[2 * p] = jnp.where(low, tile, turned).astype(BF16)
        dup[2 * p + 1] = jnp.where(low, turned, tile).astype(BF16)

    def lanes(p):
        return pl.ds(pl.multiple_of(p * 128, 128), 128)

    def copies(step):
        return [
            pltpu.make_async_remote_copy(
                src_ref=out_h.at[step, pl.ds(2 * side, 2)],
                dst_ref=in_h.at[step, pl.ds(2 - 2 * side, 2)],
                send_sem=send_sem.at[step, side],
                recv_sem=recv_sem.at[step, side],
                device_id=(x, peer),
                device_id_type=MESH,
            )
            for side, peer in ((0, left), (1, right))
        ]

    def apply(dup, xin, xout, s, p, then):
        sides = []
        for b2 in range(2):
            b = 2 * p + b2
            parts = []
            for jj in range(3):
                ca = cols_ref[2 * jj, b]
                cb = cols_ref[2 * jj + 1, b]
                parts.append(jnp.where(low, dup[ca], dup[cb]))
            parts.append(dup[cols_ref[6, b]][:, :64])
            picked = jnp.concatenate(parts, axis=1)
            sides.append(
                lax.dot_general(
                    picked, blk_ref[b], (((1,), (1,)), ((), ())), preferred_element_type=F32
                )
            )
        res = jnp.concatenate(sides, axis=1)
        new = xin[:, lanes(p)] - res + src_ref[s, :, lanes(p)].astype(F32)
        xout[:, lanes(p)] = new
        if then is not None:
            spread(new, then, p + 2)
        return new

    def arrive(step, dup):
        for e in range(2):
            spread(in_h[step, e].astype(F32), dup, e)
            spread(in_h[step, 2 + e].astype(F32), dup, npair + 2 + e)

    loads[0].wait()
    for e in range(2):
        out_h[0, e] = x0_ref[:, e * 128 : (e + 1) * 128].astype(BF16)
        q = npair - 2 + e
        out_h[0, 2 + e] = x0_ref[:, q * 128 : (q + 1) * 128].astype(BF16)
    pl.semaphore_wait(barrier, len(greeted))
    first = copies(0)
    for cp in first:
        cp.start()

    @pl.loop(0, npair)
    def _(p):
        spread(x0_ref[:, lanes(p)], dup_a, p + 2)

    loads[1].wait()
    loads[2].wait()

    @pl.loop(2, npair - 2)
    def _(p):
        apply(dup_a, x0_ref, x1_ref, 0, p, dup_b)

    for cp in first:
        cp.wait()
    arrive(0, dup_a)
    for e, p in enumerate((0, 1, npair - 2, npair - 1)):
        out_h[1, e] = apply(dup_a, x0_ref, x1_ref, 0, p, dup_b).astype(BF16)
    second = copies(1)
    for cp in second:
        cp.start()

    loads[3].wait()

    @pl.loop(2, npair - 2)
    def _(p):
        apply(dup_b, x1_ref, x2_ref, 1, p, None)

    loads[4].wait()
    for q in range(NX):
        y_ref[q] = mm3(sk_ref[:, :rows], x1_ref[:, q * 512 : (q + 1) * 512])
    for cp in second:
        cp.wait()
    arrive(1, dup_b)
    for p in (0, 1, npair - 2, npair - 1):
        apply(dup_b, x1_ref, x2_ref, 1, p, None)

    gs[...] = jnp.zeros_like(gs)
    gram = None
    for q in range(NX):
        cut = slice(q * 512, (q + 1) * 512)
        y_ref[q] += mm3(sk_ref[:, rows:], x2_ref[:, cut])
        part = mm_nt(y_ref[q], y_ref[q])
        gram = part if gram is None else gram + part

    pk1[272:, :] = jnp.zeros((48, 128), F32)
    pack(gram, gs, pk1, 0)
    steps = reduce_steps(at, pk1, 40, (l1, l2, None, lo, s1, q1), False)
    next(steps)
    bulk = exchange(lambda peer: y_ref.at[peer], lambda i: yq.at[i], NX, x, at.along_x, sb.at[0], qb.at[0])
    yq[x] = y_ref[x]
    tx[:, :120, 128:] = jnp.zeros((NX, 120, 128), F32)
    pk2[544:, :] = jnp.zeros((32, 128), F32)
    pk5[n + 144 :, :] = jnp.zeros((40, 128), F32)
    pk3[...] = jnp.zeros_like(pk3)
    pk4[...] = jnp.zeros_like(pk4)
    xr[...] = jnp.zeros_like(xr)
    d_ref[...] = jnp.zeros_like(d_ref)
    loads[5].wait()
    halves_of = [[ms_ref[level, :, n * h : n * h + n] for h in range(2)] for level in range(2)]
    ss_ref[...] = mm_nt(halves_of[1][0], halves_of[1][0]) + mm_nt(halves_of[1][1], halves_of[1][1])
    run(steps)
    unpack(lo, 0, fac, 0)
    shares = []

    def send_rows(k):
        part = (pl.ds(k * NB, NB), pl.ds(0, 128 if k < 3 else 256))
        shares.append(
            exchange(
                lambda _: fac.at[0, *part], lambda i: tx.at[i, *part], NX, x, at.along_x, st.at[k], qt.at[k]
            )
        )

    chol_inv(fac.at[pl.ds(0, 1)], 1, send_rows)
    tx[x] = fac[0]
    finish(bulk)
    for share in shares:
        finish(share)

    def send_pair(p, lo, hi, lane):
        return exchange(
            lambda _: zf_ref.at[p, x, lo:hi], lambda i: zf_ref.at[p, i, lo:hi],
            NX, x, at.along_x, sb.at[lane], qb.at[lane],
        )

    def inner_products(p, pk):
        raw = mm3_nt(x2_ref[:, :512], zf_ref[p, 0])
        for q in range(1, NX):
            raw = raw + mm3_nt(x2_ref[:, q * 512 : (q + 1) * 512], zf_ref[p, q])
        pk[:rows, :] = raw[:, :128]
        pk[rows:, :72] = raw[:, 128:]

    bulks = []
    for p in range(2):
        for h in range(2):
            u_ref[h, :, :n] = mm(halves_of[0][h], tx[2 * p + h][:, :n])
        zf_ref[p, x] = mm3(u_ref[0, :, :n], yq[2 * p]) + mm3(u_ref[1, :, :n], yq[2 * p + 1])
        if p == 0:
            bulks.append(send_pair(0, 0, n, 1))
    for p in range(2):
        pack(mm_nt(zf_ref[p, x], zf_ref[p, x]), gs, pk2, 272 * p)
    grams = reduce_steps(at, pk2, 72, (p1, p2, px, po, s2, q2), True)
    next(grams)
    pk5[:n, :] = mm_nt(zf_ref[0, x], zf_ref[1, x, :128])
    xr[:, :n] = mm_nt(zf_ref[1, x, 128:], zf_ref[0, x])
    pk5[n : n + 72, :] = xr[:, :128]
    pk5[n + 72 : n + 144, :] = xr[:, 128:]
    cross = reduce_steps(at, pk5, 48, (r1, r2, rx, ro, s5, q5), True)
    first = reduce_steps(at, pk3, 64, (c1, c2, None, co, s3, q3), False)
    second = reduce_steps(at, pk4, 64, (e1, e2, None, eo, s4, q4), False)
    next(cross)
    next(grams)
    next(cross)
    next(grams)
    bulks.append(send_pair(1, 0, 80, 2))
    finish(bulks[0])
    inner_products(0, pk3)
    next(first)
    next(grams)
    next(cross)
    bulks.append(send_pair(1, 80, n, 3))
    next(first)
    run(grams)

    for p in range(2):
        unpack(po, 272 * p, fac, p)
    keep = pltpu.make_async_copy(zf_ref, zf_hbm, in_sem.at[6])

    def during_pairs(k):
        if k == 1:
            next(cross)
        if k == 2:
            next(first)

    def during_top(k):
        if k == 2:
            next(second)
        if k == 4:
            next(second)

    chol_inv(fac, 2, during_pairs)
    for p in range(2):
        u_ref[p, :, :n] = mm(halves_of[1][p], fac[p][:, :n])
    finish(bulks[1])
    finish(bulks[2])
    keep.start()
    inner_products(1, pk4)
    next(second)
    run(first)
    run(cross)
    gs[:, :128] = ro[:n, :]
    xr[:, :128] = ro[n : n + 72, :]
    xr[:, 128:] = ro[n + 72 : n + 144, :]
    gs[:, 128:n] = xr[...].T[:n]
    d_ref[:, :n] = mm_nt(mm(u_ref[0, :, :n], gs[:, :n]), u_ref[1, :, :n])
    fac[0, :, :n] = ss_ref[...] + d_ref[:, :n] + d_ref[...].T[:n, :n]
    chol_inv(fac.at[pl.ds(0, 1)], 1, during_top)
    for p in range(2):
        u_ref[p, :, :n] = mm(fac[0][:, :n], u_ref[p, :, :n])

    def in_top(p, total):
        return mm_nt(total[:rows, :], u_ref[p, :, :128]) + mm_nt(total[rows:, :][:, :72], u_ref[p, :, 128:n])

    inner = in_top(0, co)
    run(second)
    inner = inner + in_top(1, eo)
    for p in range(2):
        co_ref[p] = mm(inner, u_ref[p, :, :n])
    keep.wait()


def merged_top(start_states, sources, blocks, cols, leaf_sketch, merge_sketch):
    rows, width = start_states.shape
    rank = leaf_sketch.shape[0]
    part = width // NX
    nblk = width // 64
    anywhere = pl.BlockSpec(memory_space=pl.ANY)
    vmem = pl.BlockSpec(memory_space=pltpu.VMEM)
    dma = pltpu.SemaphoreType.DMA

    def buf(*shape, dtype=F32):
        return pltpu.VMEM(shape, dtype)

    return pl.pallas_call(
        main_kernel,
        name="merged_top",
        out_shape=(
            jax.ShapeDtypeStruct((2, NX, rank, part), F32),
            jax.ShapeDtypeStruct((2, rows, rank), F32),
        ),
        in_specs=[anywhere] * 3 + [pl.BlockSpec(memory_space=pltpu.SMEM)] + [anywhere] * 2,
        out_specs=(anywhere, vmem),
        scratch_shapes=[
            buf(2, NX, rank, part), buf(rows, width), buf(*sources.shape, dtype=BF16), buf(*blocks.shape, dtype=BF16),
            buf(*leaf_sketch.shape), buf(*merge_sketch.shape),
            buf(rows, width), buf(rows, width), buf(NX, rank, part),
            buf(nblk + 2 * HB, rows, 128, dtype=BF16), buf(nblk + 2 * HB, rows, 128, dtype=BF16),
            buf(2, 4, rows, 128, dtype=BF16), buf(2, 4, rows, 128, dtype=BF16),
            buf(NX, rank, part), buf(rank, 256), buf(2, rank, 256), buf(2, rank, 256), buf(NX, rank, 256),
            buf(72, 256), buf(rank, rank), buf(rank, 256),
            buf(320, 128), buf(NW, 40, 128), buf(NZ, 40, 128), buf(320, 128),
            buf(576, 128), buf(NW, 72, 128), buf(NZ, 72, 128), buf(NX, 72, 128), buf(576, 128),
            buf(512, 128), buf(NW, 64, 128), buf(NZ, 64, 128), buf(512, 128),
            buf(512, 128), buf(NW, 64, 128), buf(NZ, 64, 128), buf(512, 128),
            buf(384, 128), buf(NW, 48, 128), buf(NZ, 48, 128), buf(NX, 48, 128), buf(384, 128),
            dma((7,)), dma((2, 2)), dma((2, 2)),
            dma((4, 8)), dma((4, 8)), dma((4, 8)), dma((4, 8)), dma((4, 8)), dma((4, 8)), dma((4, 8)), dma((4, 8)), dma((4, 8)), dma((4, 8)),
            dma((4, 4)), dma((4, 4)), dma((5, 4)), dma((5, 4)),
        ],
        compiler_params=pltpu.CompilerParams(
            collective_id=0, has_side_effects=True, vmem_limit_bytes=60 * 2**20
        ),
    )(start_states, sources, blocks, cols, leaf_sketch, merge_sketch)


def project_kernel(co_ref, z_ref, o_ref):
    o_ref[...] = mm3(co_ref[0], z_ref[0, 0]) + mm3(co_ref[1], z_ref[1, 0])


def project(coeffs, z):
    _, rows, rank = coeffs.shape
    parts, part = z.shape[1], z.shape[3]
    return pl.pallas_call(
        project_kernel,
        name="project",
        grid=(parts,),
        out_shape=jax.ShapeDtypeStruct((rows, parts * part), F32),
        in_specs=[
            pl.BlockSpec((2, rows, rank), lambda q: (0, 0, 0)),
            pl.BlockSpec((2, 1, rank, part), lambda q: (0, q, 0, 0)),
        ],
        out_specs=pl.BlockSpec((rows, part), lambda q: (0, q)),
        compiler_params=pltpu.CompilerParams(vmem_limit_bytes=60 * 2**20),
    )(coeffs, z)


def local(start_states, sources, blocks, columns, leaf_sketch, merge_sketch):
    cols = columns.T - lax.axis_index("cell") * blocks.shape[0] + HB
    z, coeffs = merged_top(start_states, sources, blocks, cols, leaf_sketch, merge_sketch)
    return project(coeffs, z)


def solution(mesh):
    placed = (
        P("snap", "cell"),
        P(None, "snap", "cell"),
        P("cell", None, None),
        P("cell", None),
        P(),
        P(),
    )
    return jax.shard_map(
        local, mesh=mesh, in_specs=placed, out_specs=P("snap", "cell"), check_vma=False
    )
```
